32 devices in a mesh: expert: 8 (over y, x, core), wshard: 4 (over z).
Axes of the slice: x: 2, y: 2, z: 4, core: 2. Of those that a mesh axis runs over, the one named last changes fastest.
Arguments:
- hidden_in: bfloat16 [2, 8, 256, 2048], P(None, 'expert', 'wshard'), may hold values from -6 to 6
- doc_ids: int32 [2, 8, 256], P(None, 'expert'), may hold values from 0 to 2, as said below
- routes: int32 [2, 8, 256, 8], P(None, 'expert', 'wshard'), may hold values from 0 to 15, all different within a row; in each aligned block of 64 rows (0 to 63, 64 to 127, ..., all dimensions but the last counted through in order) at most 36 rows name the same one
- attn_gain: float32 [2048], replicated, may hold values from 0.1 to 1.9
- q_gain: float32 [2048], replicated, may hold values from 0.1 to 1.9
- k_gain: float32 [2048], replicated, may hold values from 0.1 to 1.9
- ffn_gain: float32 [2048], replicated, may hold values from 0.1 to 1.9
- w_qkv: bfloat16 [2048, 6144], P('wshard'), may hold values from -0.125 to 0.125
- w_out: bfloat16 [2048, 2048], P('wshard'), may hold values from -0.5 to 0.5
- w_router: bfloat16 [2048, 16], P('wshard'), may hold values from -0.0625 to 0.0625
- w_gate_up: bfloat16 [16, 2048, 2048], P('expert', 'wshard'), may hold values from -0.125 to 0.125
- w_down: bfloat16 [16, 1024, 2048], P('expert', None, 'wshard'), may hold values from -6 to 6
- cotangent: bfloat16 [2, 8, 256, 2048], P(None, 'expert', 'wshard'), may hold values from -6 to 6
Outputs:
- hidden_out: bfloat16 [2, 8, 256, 2048], P(None, 'expert', 'wshard')
- grad_in: bfloat16 [2, 8, 256, 2048], P(None, 'expert', 'wshard')
- grad_attn_gain: float32 [2048], P(('expert', 'wshard'))
- grad_q_gain: float32 [2048], P(('expert', 'wshard'))
- grad_k_gain: float32 [2048], P(('expert', 'wshard'))
- grad_ffn_gain: float32 [2048], P(('expert', 'wshard'))
- grad_qkv: float32 [2048, 6144], P(('expert', 'wshard'))
- grad_out_proj: float32 [2048, 2048], P(('expert', 'wshard'))
- grad_router: float32 [2048, 16], P(('expert', 'wshard'))
- grad_gate_up: float32 [16, 2048, 2048], P('expert', 'wshard')
- grad_down: float32 [16, 1024, 2048], P('expert', None, 'wshard')
The draws below stay inside these ranges and needn't reach their ends.
Inputs may be any that keep to these rules, and one draw needn't show every extreme that they name: `doc_ids`: along a sequence the numbers never fall and take 0, 1 and 2: document 0 ends within the first 32 positions, document 2 begins within the last 32 positions. `routes`: each row names 8 different experts. In each aligned block of 64 rows (one device's rows of one micro-batch) no expert is named by more than 36 rows, and in some blocks one is named by exactly 36.
All inputs are finite; a program needn't handle non-finite values.
Results may differ from the reference program's by a relative error of at most 0.02.
Values may be sent and summed in bfloat16 or wider, within the bound.
No kernel may reach another device: no remote copies, remote signals or barrier semaphores. Data moves between devices by JAX's collectives and lax.ppermute only.
A program may use at most 384 MiB of HBM per device.

```python
import math
import jax
import jax.numpy as jnp
import numpy as np
from jax import lax

D = 2048
HEADS = 16
HEAD_DIM = 128
FF = 1024
TOP = 8
MICRO = 2
TOK_DEV = 64
EXPERTS = 16
SEQ = 256
SEQS = 8
CAP = 36
N_WSHARD = 4


def draw_doc_ids(key, part):
    key = jax.random.fold_in(key, 11)
    first_key, last_key = jax.random.split(key)
    shape = (MICRO, SEQS, 1)
    begin = jax.random.randint(first_key, shape, 1, TOK_DEV // 2 + 1)
    finish = jax.random.randint(last_key, shape, SEQ - TOK_DEV // 2, SEQ)
    position = jnp.arange(SEQ, dtype=jnp.int32)[None, None, :]
    return (position >= begin).astype(jnp.int32) + (position >= finish).astype(jnp.int32)


def steps_of(rng, extent, cuts, least, largest):
    factor_of, own = 1.0, jax.random.fold_in(rng, 6)
    for axis_at, blocks in cuts:
        steps = jnp.exp(jax.random.uniform(jax.random.fold_in(own, axis_at), (blocks,), jnp.float32, least / len(cuts), largest / len(cuts)))
        factor_of = factor_of * jnp.repeat(steps, extent[axis_at] // blocks).reshape([-1 if axis == axis_at else 1 for axis in range(len(extent))])
    return factor_of


def shared_out(key, own, number, rows, number_of, top, most, lean):
    order = jax.random.permutation(key, number_of)
    packed, usual = portions_of(number_of, rows * top, most, lean, True), portions_of(number_of, rows * top, most, lean, False)
    places = jnp.arange(number_of)

    def named(lengths, rotation):
        used = int((lengths > 0).sum())
        fixed = max(1, used // 4)
        moved = fixed + (places - fixed + rotation * (used - fixed)) % max(1, number_of - fixed)
        return jnp.zeros((number_of,), jnp.int32).at[order[jnp.where(places < fixed, places, moved)]].set(jnp.asarray(lengths, jnp.int32))

    lengths = jnp.where(number % 4 == 0, named(packed, number // 4), named(usual, number - number // 4 - 1))
    mixed = jax.random.permutation(jax.random.fold_in(own, 3), number_of)
    donor, taker = mixed[0:number_of // 2 * 2:2], mixed[1:number_of // 2 * 2:2]
    slack = jnp.minimum(lengths[donor] - 1, most - lengths[taker]) // 2
    slack = jnp.where((donor == order[0]) | (taker == order[0]) | (lengths[taker] == 0), 0, jnp.maximum(slack, 0))
    moved = jax.random.randint(jax.random.fold_in(own, 4), (number_of // 2,), 0, 1 << 20) % (slack + 1)
    lengths = lengths.at[donor].add(-moved).at[taker].add(moved)
    labels = jnp.searchsorted(jnp.cumsum(lengths), jnp.arange(rows * top), side="right").astype(jnp.int32)
    listing = labels.reshape(top, rows).T
    listing = listing[jax.random.permutation(jax.random.fold_in(own, 1), rows)]
    rotation = jax.random.randint(jax.random.fold_in(own, 2), (rows, 1), 0, top)
    return jnp.take_along_axis(listing, (jnp.arange(top)[None, :] + rotation) % top, axis=1)


def portions_of(amount, total, reach, skew, full):
    portions = [(1 << 20) // math.isqrt(grade ** skew) + 1 for grade in range(1, amount + 1)]
    largest = reach if full else min(reach, max(-(-total // amount), total * portions[0] // sum(portions)))
    least = 1 if total - largest >= amount - 1 else 0
    given, rest = [largest] + [least] * (amount - 1), total - largest - least * (amount - 1)
    while rest > 0:
        candidates = [i for i in range(1, amount) if given[i] < largest] or [i for i in range(1, amount) if given[i] < reach]
        pool, budget = sum([portions[i] for i in candidates]), rest
        for i in candidates:
            extra = min(reach - given[i], max(1, budget * portions[i] // pool), rest)
            given[i] = given[i] + extra
            rest = rest - extra
    return np.array(given)


def bell_draw(stream_key, shape, scale, reach, cuts=(), kind=jnp.bfloat16):
    factor_of = steps_of(stream_key, shape, cuts, -0.22, 0.18) if cuts else 1.0
    drawn = jax.random.normal(stream_key, shape, jnp.float32) * scale * factor_of
    return jnp.minimum(jnp.maximum(drawn, -reach), reach).astype(kind)


def setup_inputs(seed: int = 0) -> dict:
    key_list = jax.random.split(jax.random.key(seed), 14)
    hidden_in = bell_draw(key_list[0], (MICRO, SEQS, SEQ, D), 1.0, 6.0, ((1, 8), (2, 4)))
    doc_ids = draw_doc_ids(jax.random.fold_in(key_list[13], 71), 0)
    routes_keys = jax.random.split(jax.random.fold_in(key_list[2], 1), MICRO * SEQS * SEQ // TOK_DEV)
    routes_turns = jax.random.permutation(jax.random.fold_in(key_list[2], 3), MICRO * SEQS * SEQ // TOK_DEV)
    routes = jax.vmap(lambda own, number: shared_out(jax.random.fold_in(key_list[2], 2), own, number, TOK_DEV, EXPERTS, TOP, CAP, 2))(routes_keys, routes_turns).reshape((MICRO, SEQS, SEQ, TOP))
    attn_gain = jnp.clip(1.0 + 0.18 * jax.random.normal(key_list[3], (D,), jnp.float32), 0.1, 1.9)
    q_gain = jnp.clip(1.0 + 0.18 * jax.random.normal(key_list[4], (D,), jnp.float32), 0.1, 1.9)
    k_gain = jnp.clip(1.0 + 0.18 * jax.random.normal(key_list[5], (D,), jnp.float32), 0.1, 1.9)
    ffn_gain = jnp.clip(1.0 + 0.18 * jax.random.normal(key_list[6], (D,), jnp.float32), 0.1, 1.9)
    w_qkv = bell_draw(key_list[7], (D, 3 * D), D ** -0.5, 0.125, ((0, 4),))
    w_out = bell_draw(key_list[8], (D, D), (D // 16) ** -0.5, 0.5, ((0, 4),))
    w_router = bell_draw(key_list[9], (D, EXPERTS), (4 * D) ** -0.5, 0.0625, ((0, 4),))
    w_gate_up = bell_draw(key_list[10], (EXPERTS, D, 2 * FF), D ** -0.5, 0.125, ((0, 8), (1, 4)))
    w_down = bell_draw(key_list[11], (EXPERTS, FF, D), 1.0, 6.0, ((0, 8), (2, 4)))
    cotangent = bell_draw(key_list[12], (MICRO, SEQS, SEQ, D), 1.0, 6.0, ((1, 8), (2, 4)))
    return dict(hidden_in=hidden_in, doc_ids=doc_ids, routes=routes, attn_gain=attn_gain, q_gain=q_gain, k_gain=k_gain, ffn_gain=ffn_gain, w_qkv=w_qkv, w_out=w_out, w_router=w_router, w_gate_up=w_gate_up, w_down=w_down, cotangent=cotangent)


@jax.custom_vjp
def low(v):
    return lax.optimization_barrier(v.astype(jnp.bfloat16)).astype(jnp.float32)

@jax.custom_vjp
def low_back(v):
    return v

def low_keep(v):
    return (low(v), None)

def low_pass(kept, grad):
    return (grad,)

def back_keep(v):
    return (v, None)

def back_low(kept, grad):
    return (low(grad),)
low.defvjp(low_keep, low_pass)
low_back.defvjp(back_keep, back_low)
EPS = 1e-05
THETA = 10000.0
HIGH = lax.Precision.HIGHEST

def rms_scale(values):
    return lax.rsqrt(lax.optimization_barrier(jnp.mean(values * values, axis=-1, keepdims=True)) + EPS)

def rotary_tables(count, head_size):
    half = head_size // 2
    freq = THETA ** (-(jnp.arange(half, dtype=jnp.float32) * 2.0 / head_size))
    angle = jnp.arange(count, dtype=jnp.float32)[:, None] * freq[None, :]
    return (jnp.cos(angle)[:, None, :], jnp.sin(angle)[:, None, :])

def rotate(values, cosine, sine):
    half = values.shape[-1] // 2
    first = values[..., :half]
    second = values[..., half:]
    return jnp.concatenate([first * cosine - second * sine, second * cosine + first * sine], axis=-1)

def slot_tables(choose):
    blocks = choose.shape[0] * N_WSHARD
    per_block = TOK_DEV * TOP
    flat_ids = choose.reshape(blocks, per_block)
    hot = (flat_ids[..., None] == jnp.arange(EXPERTS, dtype=jnp.int32)).astype(jnp.int32)
    rank = lax.optimization_barrier(jnp.sum((jnp.cumsum(hot, axis=1) - hot) * hot, axis=-1))
    slot = jnp.arange(blocks, dtype=jnp.int32)[:, None] * CAP + rank
    token = (jnp.arange(blocks * per_block, dtype=jnp.int32) // TOP).reshape(blocks, per_block)
    table = jnp.full((EXPERTS, blocks * CAP), blocks * TOK_DEV, jnp.int32)
    table = table.at[flat_ids.reshape(-1), slot.reshape(-1)].set(token.reshape(-1))
    place = flat_ids * (blocks * CAP) + slot
    return (table, place.reshape(-1, TOP))

def layer_group(params, inputs):
    attn_gain, q_gain, k_gain, ffn_gain, w_qkv, w_out, w_router, w_gate_up, w_down = params
    tokens, docs, choose = inputs
    bundle = tokens.shape[0]
    cosine, sine = rotary_tables(SEQ, HEAD_DIM)
    normed = low(tokens * rms_scale(tokens) * attn_gain)
    projected = low_back(jnp.einsum('bsd,de->bse', normed, w_qkv, precision=HIGH))
    query_raw = projected[..., :D]
    key_raw = projected[..., D:2 * D]
    value_raw = projected[..., 2 * D:]
    query_hat = (query_raw * rms_scale(query_raw) * q_gain).reshape(bundle, SEQ, HEADS, HEAD_DIM)
    key_hat = (key_raw * rms_scale(key_raw) * k_gain).reshape(bundle, SEQ, HEADS, HEAD_DIM)
    queries = low(rotate(query_hat, cosine, sine))
    keys = low(rotate(key_hat, cosine, sine))
    values = low(value_raw.reshape(bundle, SEQ, HEADS, HEAD_DIM))
    raw = jnp.einsum('bqhd,bkhd->bhqk', queries, keys, precision=HIGH) * HEAD_DIM ** (-0.5)
    scores = low_back(raw)
    position = jnp.arange(SEQ, dtype=jnp.int32)
    allowed = (position[None, :] <= position[:, None])[None] & (docs[:, :, None] == docs[:, None, :])
    scores = jnp.where(allowed[:, None], scores, -1e+30)
    probs = low(jax.nn.softmax(scores, axis=-1))
    attended = low_back(low(jnp.einsum('bhqk,bkhd->bqhd', probs, values, precision=HIGH)))
    attended = attended.reshape(bundle, SEQ, D)
    resid = tokens + low_back(jnp.einsum('bsd,de->bse', attended, w_out, precision=HIGH))
    ffn_in = low(resid * rms_scale(resid) * ffn_gain)
    logits = low_back(jnp.einsum('bsd,de->bse', ffn_in, w_router, precision=HIGH))
    gate_all = jax.nn.softmax(logits, axis=-1).reshape(bundle * SEQ, EXPERTS)
    gates = jnp.take_along_axis(gate_all, choose.reshape(bundle * SEQ, TOP), axis=1)
    table, place = slot_tables(choose)
    padded = jnp.concatenate([ffn_in.reshape(bundle * SEQ, D), jnp.zeros((1, D), ffn_in.dtype)], axis=0)
    rows = low_back(padded[table])
    gate_up = low_back(jnp.einsum('erd,edf->erf', rows, w_gate_up, precision=HIGH))
    act = low(jax.nn.silu(gate_up[..., :FF]) * gate_up[..., FF:])
    expert_out = low_back(low(jnp.einsum('erf,efd->erd', act, w_down, precision=HIGH)))
    picked = expert_out.reshape(-1, D)[place]
    mixture = lax.optimization_barrier(jnp.sum(gates[..., None] * picked, axis=1))
    return resid + mixture.reshape(bundle, SEQ, D)

def reference(hidden_in, doc_ids, routes, attn_gain, q_gain, k_gain, ffn_gain, w_qkv, w_out, w_router, w_gate_up, w_down, cotangent):
    bundle = 8
    groups = MICRO * SEQS // bundle
    start = hidden_in.astype(jnp.float32).reshape(groups, bundle, SEQ, D)
    docs = doc_ids.reshape(groups, bundle, SEQ)
    choose = routes.reshape(groups, bundle, SEQ, TOP)
    params = (attn_gain.astype(jnp.float32), q_gain.astype(jnp.float32), k_gain.astype(jnp.float32), ffn_gain.astype(jnp.float32), w_qkv.astype(jnp.float32), w_out.astype(jnp.float32), w_router.astype(jnp.float32), w_gate_up.astype(jnp.float32), w_down.astype(jnp.float32))
    group_step = jax.checkpoint(layer_group)

    def forward(inputs, weights):

        def scan_step(carry, pieces):
            return (carry, group_step(weights, pieces))
        unused, outputs = lax.scan(scan_step, jnp.zeros((), jnp.float32), (inputs, docs, choose))
        return outputs
    outputs, pullback = jax.vjp(forward, start, params)
    input_grad, weight_grads = pullback(cotangent.astype(jnp.float32).reshape(groups, bundle, SEQ, D))
    full_shape = (MICRO, SEQS, SEQ, D)
    return (outputs.reshape(full_shape).astype(jnp.bfloat16), input_grad.reshape(full_shape).astype(jnp.bfloat16), weight_grads[0], weight_grads[1], weight_grads[2], weight_grads[3], weight_grads[4], weight_grads[5], weight_grads[6], weight_grads[7], weight_grads[8])
```

```python
import jax
import jax.numpy as jnp
from jax import lax
from jax.sharding import PartitionSpec as P

HEADS = 16
EPS = 1e-05
THETA = 10000.0
AXES = ("expert", "wshard")
LOW = jnp.bfloat16
F32 = jnp.float32


def rms_scale(values):
    return lax.rsqrt(jnp.mean(values * values, axis=-1, keepdims=True) + EPS)


def rotate(values, cosine, sine):
    half = values.shape[-1] // 2
    first = values[..., :half]
    second = values[..., half:]
    return jnp.concatenate(
        [first * cosine - second * sine, second * cosine + first * sine], axis=-1
    )


def norm_back(values, scale, gain, grads, inner):
    weighted = gain * grads
    return scale * weighted - values * scale * scale * scale * inner


def dot(a, b, dims):
    return lax.dot_general(a, b, (dims, ((), ())), preferred_element_type=F32)


def mm(a, b):
    return dot(a, b, ((1,), (0,)))


def mm_t(a, b):
    return dot(a, b, ((1,), (1,)))


def t_mm(a, b):
    return dot(a, b, ((0,), (0,)))


def build(n_e, n_w):
    bits = [1 << b for b in range(n_e.bit_length() - 1)]
    plane = bits[1:]
    nd = len(plane)

    def swap(x, d):
        return lax.ppermute(x, "expert", [(i, i ^ d) for i in range(n_e)])

    def shift(x, s):
        return lax.ppermute(x, "wshard", [(j, (j + s) % n_w) for j in range(n_w)])

    def joint(x, pairs):
        return lax.ppermute(x, AXES, pairs)

    def line_gather(x):
        return [x] + [shift(x, n_w - r) for r in range(1, n_w)]

    def line_scatter(blocks):
        total = blocks[0].astype(F32)
        for r in range(1, n_w):
            total = total + shift(blocks[r], r).astype(F32)
        return total

    def line_sum(x, shard):
        x = jnp.roll(x.reshape(2, n_w, -1), shard, axis=1)
        return jnp.roll(lax.psum(x, "wshard"), -shard, axis=1)

    def part_of(r):
        return r * nd // n_w

    def order(r):
        p = part_of(r)
        return [plane[(s + p) % nd] for s in range(nd)]

    def plane_gather(blocks):
        groups = [{(r, 0): b for r, b in enumerate(blocks)}]
        held = dict(groups[0])
        for step in range(nd):
            got = {}
            for (r, m), b in held.items():
                d = order(r)[step]
                got[(r, m | d)] = swap(b, d)
            held.update(got)
            groups.append(got)
        return groups

    def plane_scatter(parts):
        parts = dict(parts)
        for step in reversed(range(nd)):
            for r in range(n_w):
                d = order(r)[step]
                for r2, m in sorted(k for k in parts if k[0] == r and k[1] & d):
                    got = swap(parts.pop((r, m)), d).astype(F32)
                    keep = parts[(r, m ^ d)].astype(F32)
                    parts[(r, m ^ d)] = (keep + got).astype(LOW)
        return [parts[(r, 0)] for r in range(n_w)]

    def hyper_scatter(x, me, dims, kind):
        x = x.reshape((2,) * len(bits) + x.shape[1:])
        left = list(reversed(bits))
        for d in dims:
            at = left.index(d)
            bit = (me // d) % 2
            send = lax.dynamic_index_in_dim(x, 1 - bit, at, keepdims=False).astype(kind)
            keep = lax.dynamic_index_in_dim(x, bit, at, keepdims=False)
            x = (keep.astype(F32) + swap(send, d).astype(F32)).astype(kind)
            left.pop(at)
        return x

    def local(
        hidden_in,
        doc_ids,
        routes,
        attn_gain,
        q_gain,
        k_gain,
        ffn_gain,
        w_qkv,
        w_out,
        w_router,
        w_gate_up,
        w_down,
        cotangent,
    ):
        micro = hidden_in.shape[0]
        rows = hidden_in.shape[2]
        width = hidden_in.shape[3]
        heads = HEADS
        head = width // heads
        my_heads = heads // n_w
        cols = width // n_w
        experts = w_router.shape[1]
        local_experts = w_gate_up.shape[0]
        units = w_down.shape[1]
        own = micro * rows
        seq = n_w * rows
        me = lax.axis_index("expert")
        shard = lax.axis_index("wshard")
        core = me % 2
        my_expert = (me // 2) * n_w + shard
        scale = head ** (-0.5)

        piece = width // n_w // n_e
        mine = lax.dynamic_slice_in_dim(w_qkv, me * piece, piece, 0)
        mine = mine.reshape(piece, 3, n_w, cols)

        def columns_for(target):
            return lax.dynamic_index_in_dim(mine, target % n_w, 2, keepdims=False)

        bank = jnp.zeros((n_w, piece, 3, cols), LOW)
        for s in range(n_w):
            got = columns_for(shard + s)
            if s:
                got = shift(got, s)
            bank = lax.dynamic_update_index_in_dim(bank, got, (shard - s + n_w) % n_w, 0)
        bank = bank.reshape(n_w, piece, 3 * cols)
        w_heads = jnp.zeros((n_w, n_e, piece, 3 * cols), LOW)
        half = piece // 2
        for p in range(2):
            dims = plane[p:] + plane[:p] + [1]
            held = {0: bank[:, p * half : (p + 1) * half]}
            for d in dims:
                held.update({m | d: swap(b, d) for m, b in list(held.items())})
            for m, b in held.items():
                w_heads = lax.dynamic_update_slice(
                    w_heads, b[:, None], (0, jnp.bitwise_xor(me, m), p * half, 0)
                )
        w_heads = w_heads.reshape(width, 3 * cols)

        tokens = hidden_in.reshape(own, width).astype(F32)
        scale_one = rms_scale(tokens)
        normed = (tokens * scale_one * attn_gain).astype(LOW)
        normed_all = jnp.concatenate(line_gather(normed), 0)

        router = lax.all_gather(w_router, "wshard", axis=0, tiled=True)
        all_routes = lax.all_gather(routes.reshape(own, -1), AXES, axis=0, tiled=False)

        half_rows = w_gate_up.shape[1] // 2
        half_units = units // 2

        def expert_pairs(s, h):
            out = []
            for c in range(n_e // 2):
                for w in range(n_w):
                    t = (w + s) % n_w
                    src = ((2 * c + t // local_experts) * n_w + w, (2 * c + h) * n_w + t)
                    if src[0] != src[1]:
                        out.append(src)
            return out

        holder = shard // local_experts
        up_own, down_own = [], []
        for s in range(n_w):
            target = (shard + s) % n_w
            j = jnp.clip(target - local_experts * core, 0, local_experts - 1)
            up_got = jnp.zeros((half_rows, 2 * units), LOW)
            down_got = jnp.zeros((half_units, cols), LOW)
            up_src = lax.dynamic_index_in_dim(w_gate_up, j, 0, keepdims=False)
            down_src = lax.dynamic_index_in_dim(w_down, j, 0, keepdims=False)
            for h in range(2):
                up_h = up_src[h * half_rows : (h + 1) * half_rows]
                down_h = down_src[h * half_units : (h + 1) * half_units]
                up_in = joint(up_h, expert_pairs(s, h))
                down_in = joint(down_h, expert_pairs(s, h))
                if s == 0:
                    up_in = jnp.where(holder == h, up_h, up_in)
                    down_in = jnp.where(holder == h, down_h, down_in)
                up_got = jnp.where(core == h, up_in, up_got)
                down_got = jnp.where(core == h, down_in, down_got)
            up_own.append(up_got)
            down_own.append(down_got)
        w_up = jnp.zeros((n_w, 2, half_rows, 2 * units), LOW)
        w_dn = jnp.zeros((2, half_units, n_w, cols), LOW)
        for s in range(n_w):
            w = (shard - s + n_w) % n_w
            for which, up_b, down_b in (
                (core, up_own[s], down_own[s]),
                (1 - core, swap(up_own[s], 1), swap(down_own[s], 1)),
            ):
                w_up = lax.dynamic_update_slice(w_up, up_b[None, None], (w, which, 0, 0))
                w_dn = lax.dynamic_update_slice(w_dn, down_b[None, :, None], (which, 0, w, 0))
        w_up = w_up.reshape(width, 2 * units)
        w_dn = w_dn.reshape(units, width)

        projected = mm(normed_all, w_heads)
        raw = projected.reshape(n_w, micro, rows, 3, my_heads, head)
        squares = jnp.sum(projected.reshape(-1, 3, cols)[:, :2] ** 2, axis=-1).T
        scales = lax.rsqrt(line_sum(squares, shard) / width + EPS)
        scales = scales.reshape(2, n_w, micro, rows, 1, 1)
        gain_q = lax.dynamic_slice_in_dim(q_gain, shard * cols, cols).reshape(my_heads, head)
        gain_k = lax.dynamic_slice_in_dim(k_gain, shard * cols, cols).reshape(my_heads, head)
        block_at = (shard + jnp.arange(n_w, dtype=jnp.int32)) % n_w
        positions = (
            block_at[:, None] * rows + jnp.arange(rows, dtype=jnp.int32)[None, :]
        )
        freq = THETA ** (-(jnp.arange(head // 2, dtype=F32) * 2.0 / head))
        angle = positions.astype(F32)[:, None, :, None, None] * freq
        cosine, sine = jnp.cos(angle), jnp.sin(angle)
        q_raw, k_raw, v_raw = raw[..., 0, :, :], raw[..., 1, :, :], raw[..., 2, :, :]
        queries = rotate(q_raw * scales[0] * gain_q, cosine, sine).astype(LOW)
        keys = rotate(k_raw * scales[1] * gain_k, cosine, sine).astype(LOW)
        values = v_raw.astype(LOW)

        def by_head(x):
            return x.transpose(1, 3, 0, 2, 4).reshape(micro * my_heads, seq, head)

        def by_token(x):
            x = x.reshape(micro, my_heads, n_w, rows, head)
            return x.transpose(2, 0, 3, 1, 4)

        q_h, k_h, v_h = by_head(queries), by_head(keys), by_head(values)
        flat_pos = positions.reshape(seq)
        docs = jnp.take(doc_ids[:, 0], flat_pos, axis=1)
        allowed = (flat_pos[None, :] <= flat_pos[:, None])[None] & (
            docs[:, :, None] == docs[:, None, :]
        )
        allowed = jnp.repeat(allowed, my_heads, axis=0)
        scores = jnp.einsum("bqd,bkd->bqk", q_h, k_h, preferred_element_type=F32) * scale
        scores = jnp.where(allowed, scores, -1e30)
        peak = jnp.max(scores, axis=-1, keepdims=True)
        expo = jnp.exp(scores - peak)
        probs = expo / jnp.sum(expo, axis=-1, keepdims=True)
        probs_low = probs.astype(LOW)
        attended = jnp.einsum("bqk,bkd->bqd", probs_low, v_h, preferred_element_type=F32)
        attended = by_token(attended.astype(LOW)).reshape(n_w * own, cols)
        branch = mm(attended, w_out).astype(LOW).reshape(n_w, own, width)
        resid = tokens + line_scatter([branch[r] for r in range(n_w)])

        scale_two = rms_scale(resid)
        ffn_in = (resid * scale_two * ffn_gain).astype(LOW)
        upstream = cotangent.reshape(own, width)
        x_groups = plane_gather(line_gather(ffn_in))
        dy_groups = plane_gather(line_gather(upstream))
        used = jnp.any(all_routes == my_expert, axis=-1)

        mix_parts, back_parts = {}, {}
        grad_up = jnp.zeros((width, 2 * units), F32)
        grad_dn = jnp.zeros((units, width), F32)
        grad_router = jnp.zeros((width, experts), F32)
        hot = jnp.arange(experts, dtype=jnp.int32)[None, :] == my_expert
        for x_group, dy_group in zip(x_groups, dy_groups):
            names = list(x_group)
            x = jnp.concatenate([x_group[n] for n in names], 0)
            dy = jnp.concatenate([dy_group[n] for n in names], 0)
            owner = jnp.stack(
                [jnp.bitwise_xor(me, m) * n_w + (shard + r) % n_w for r, m in names]
            )
            mask = jnp.take(used, owner, axis=0).reshape(-1, 1)
            gate_all = jax.nn.softmax(mm(x, router), axis=-1)
            gate = jnp.sum(jnp.where(hot, gate_all, 0.0), axis=-1, keepdims=True)
            gate = jnp.where(mask, gate, 0.0)
            gate_up = mm(x, w_up)
            g, u = gate_up[:, :units], gate_up[:, units:]
            sigma = jax.nn.sigmoid(g)
            silu = g * sigma
            act = (silu * u).astype(LOW).astype(F32)
            lifted = mm_t(dy, w_dn)
            dgate = jnp.sum(act * lifted, axis=-1, keepdims=True)
            act_gated = (act * gate).astype(LOW)
            dact = lifted * gate
            dgu = jnp.concatenate(
                [dact * u * (sigma * (1.0 + g * (1.0 - sigma))), dact * silu], axis=-1
            ).astype(LOW)
            dlogits = (dgate * gate * (jnp.where(hot, 1.0, 0.0) - gate_all)).astype(LOW)
            mix = mm(act_gated, w_dn).astype(LOW)
            back = (mm_t(dgu, w_up) + mm_t(dlogits, router)).astype(LOW)
            for at, name in enumerate(names):
                mix_parts[name] = mix[at * own : (at + 1) * own]
                back_parts[name] = back[at * own : (at + 1) * own]
            grad_up = grad_up + t_mm(x, dgu)
            grad_dn = grad_dn + t_mm(act_gated, dy)
            grad_router = grad_router + t_mm(x, dlogits)
        dffn = line_scatter(plane_scatter(back_parts))
        mixture = line_scatter(plane_scatter(mix_parts))
        hidden_out = (resid + mixture).astype(LOW)

        def pair_sum(x, axis):
            send = lax.dynamic_index_in_dim(x, 1 - core, axis, keepdims=False).astype(LOW)
            keep = lax.dynamic_index_in_dim(x, core, axis, keepdims=False)
            return (keep + swap(send, 1).astype(F32)).astype(LOW)

        up_sum = pair_sum(grad_up.reshape(n_w, 2, half_rows, 2 * units), 1)
        dn_sum = pair_sum(grad_dn.reshape(2, half_units, n_w, cols), 0)

        def grad_pairs(s, h):
            out = []
            for c in range(n_e // 2):
                for w in range(n_w):
                    pair = (
                        (2 * c + h) * n_w + w,
                        (2 * c + w // local_experts) * n_w + (w + s) % n_w,
                    )
                    if pair[0] != pair[1]:
                        out.append(pair)
            return out

        up_out = [[0.0, 0.0] for j in range(local_experts)]
        dn_out = [[0.0, 0.0] for j in range(local_experts)]
        for s in range(n_w):
            target = (shard + s) % n_w
            up_send = lax.dynamic_index_in_dim(up_sum, target, 0, keepdims=False)
            dn_send = lax.dynamic_index_in_dim(dn_sum, target, 1, keepdims=False)
            for h in range(2):
                up_in = joint(up_send, grad_pairs(s, h))
                dn_in = joint(dn_send, grad_pairs(s, h))
                if s == 0:
                    kept = (core == h) & (holder == core)
                    up_in = jnp.where(kept, up_send, up_in)
                    dn_in = jnp.where(kept, dn_send, dn_in)
                for j in range(local_experts):
                    right = (shard - local_experts * core - j - s) % n_w == 0
                    up_out[j][h] = jnp.where(right, up_in.astype(F32), up_out[j][h])
                    dn_out[j][h] = jnp.where(right, dn_in.astype(F32), dn_out[j][h])
        out_gate_up = jnp.stack([jnp.concatenate(u, 0) for u in up_out])
        out_down = jnp.stack([jnp.concatenate(d, 0) for d in dn_out])

        upstream = upstream.astype(F32)
        weighted = ffn_gain * dffn
        inner = jnp.mean(resid * weighted, axis=-1, keepdims=True)
        dresid = upstream + norm_back(resid, scale_two, ffn_gain, dffn, inner)
        grad_ffn_gain = jnp.sum(dffn * resid * scale_two, axis=0)
        dbranch = jnp.concatenate(line_gather(dresid.astype(LOW)), 0)
        grad_out = t_mm(attended, dbranch)
        dattended = mm_t(dbranch, w_out).astype(LOW)
        datt_h = by_head(dattended.reshape(n_w, micro, rows, my_heads, head))
        dprobs = jnp.einsum("bqd,bkd->bqk", datt_h, v_h, preferred_element_type=F32)
        probs = jnp.where(allowed, probs, 0.0)
        dscores = probs * (dprobs - jnp.sum(probs * dprobs, axis=-1, keepdims=True))
        dscores = dscores.astype(LOW)
        dq = jnp.einsum("bqk,bkd->bqd", dscores, k_h, preferred_element_type=F32) * scale
        dk = jnp.einsum("bqk,bqd->bkd", dscores, q_h, preferred_element_type=F32) * scale
        dv = jnp.einsum("bqk,bqd->bkd", probs_low, datt_h, preferred_element_type=F32)
        dq = rotate(by_token(dq), cosine, -sine)
        dk = rotate(by_token(dk), cosine, -sine)
        dv = by_token(dv)
        inners = jnp.stack(
            [
                jnp.sum(q_raw * gain_q * dq, axis=(-2, -1)),
                jnp.sum(k_raw * gain_k * dk, axis=(-2, -1)),
            ]
        )
        inners = line_sum(inners, shard) / width
        inners = inners.reshape(2, n_w, micro, rows, 1, 1)
        dq_raw = norm_back(q_raw, scales[0], gain_q, dq, inners[0])
        dk_raw = norm_back(k_raw, scales[1], gain_k, dk, inners[1])
        grad_q = jnp.sum(dq * q_raw * scales[0], axis=(0, 1, 2)).reshape(cols)
        grad_k = jnp.sum(dk * k_raw * scales[1], axis=(0, 1, 2)).reshape(cols)
        dproj = jnp.stack([dq_raw, dk_raw, dv], axis=3).astype(LOW)
        dproj = dproj.reshape(n_w * own, 3 * cols)
        dnormed = mm_t(dproj, w_heads).astype(LOW).reshape(n_w, own, width)
        dnormed = line_scatter([dnormed[r] for r in range(n_w)])
        inner = jnp.mean(tokens * (attn_gain * dnormed), axis=-1, keepdims=True)
        dx = norm_back(tokens, scale_one, attn_gain, dnormed, inner)
        grad_in = (dresid + dx).astype(LOW)
        grad_attn_gain = jnp.sum(dnormed * tokens * scale_one, axis=0)
        grad_qkv = t_mm(normed_all, dproj)

        small = width // (n_e * n_w)
        core_first = [1] + plane
        qkv = hyper_scatter(grad_qkv.reshape(n_e, n_w * small, 3 * cols), me, core_first, LOW)
        qkv = qkv.reshape(n_w, small, 3, cols)
        out_qkv = jnp.zeros((small, 3, n_w, cols), F32)
        for s in range(n_w):
            got = lax.dynamic_index_in_dim(qkv, (shard + s) % n_w, 0, keepdims=False)
            if s:
                got = shift(got, s)
            out_qkv = lax.dynamic_update_index_in_dim(
                out_qkv, got.astype(F32), (shard - s + n_w) % n_w, 2
            )
        out_qkv = out_qkv.reshape(small, 3 * width)
        to_rows = [
            (i * n_w + w, w * n_e + i) for i in range(n_e) for w in range(n_w)
        ]
        out_rows = hyper_scatter(grad_out.reshape(n_e, small, width), me, core_first, LOW)
        out_rows = joint(out_rows, to_rows).astype(F32)
        gains = jnp.stack([grad_q, grad_k]).reshape(2, n_e, small).transpose(1, 0, 2)
        gains = joint(hyper_scatter(gains, me, core_first, F32), to_rows)
        pack = jnp.concatenate([grad_router.T, grad_attn_gain[None], grad_ffn_gain[None]], 0)
        pack = pack.reshape(experts + 2, n_e, n_w * small).transpose(1, 0, 2)
        pack = hyper_scatter(pack, me, core_first, F32)
        pack = pack.reshape(experts + 2, n_w, small)
        total = 0.0
        for s in range(n_w):
            got = lax.dynamic_index_in_dim(pack, (shard + s) % n_w, 1, keepdims=False)
            total = total + (shift(got, s) if s else got)
        return (
            hidden_out.reshape(micro, 1, rows, width),
            grad_in.reshape(micro, 1, rows, width),
            total[experts],
            gains[0],
            gains[1],
            total[experts + 1],
            out_qkv,
            out_rows,
            total[:experts].T,
            out_gate_up,
            out_down,
        )

    return local


def solution(mesh):
    in_specs = (
        P(None, "expert", "wshard", None),
        P(None, "expert", None),
        P(None, "expert", "wshard", None),
        P(),
        P(),
        P(),
        P(),
        P("wshard", None),
        P("wshard", None),
        P("wshard", None),
        P("expert", "wshard", None),
        P("expert", None, "wshard"),
        P(None, "expert", "wshard", None),
    )
    out_specs = (
        P(None, "expert", "wshard", None),
        P(None, "expert", "wshard", None),
        P(("expert", "wshard")),
        P(("expert", "wshard")),
        P(("expert", "wshard")),
        P(("expert", "wshard")),
        P(("expert", "wshard"), None),
        P(("expert", "wshard"), None),
        P(("expert", "wshard"), None),
        P("expert", "wshard", None),
        P("expert", None, "wshard"),
    )
    local = build(mesh.shape["expert"], mesh.shape["wshard"])
    return jax.shard_map(local, mesh=mesh, in_specs=in_specs, out_specs=out_specs, check_vma=False)
```

```python
import jax
import jax.numpy as jnp
from jax import lax
from jax.sharding import PartitionSpec as P

HEADS = 16
EPS = 1e-05
THETA = 10000.0
ROUND_TOKENS = 2048
AXES = ("expert", "wshard")
LOW = jnp.bfloat16
F32 = jnp.float32


def rms_scale(values):
    return lax.rsqrt(jnp.mean(values * values, axis=-1, keepdims=True) + EPS)


def rotate(values, cosine, sine):
    half = values.shape[-1] // 2
    first = values[..., :half]
    second = values[..., half:]
    return jnp.concatenate(
        [first * cosine - second * sine, second * cosine + first * sine], axis=-1
    )


def norm_back(values, scale, gain, grads, inner):
    weighted = gain * grads
    return scale * weighted - values * scale * scale * scale * inner


def dot(a, b, dims):
    return lax.dot_general(a, b, (dims, ((), ())), preferred_element_type=F32)


def mm(a, b):
    return dot(a, b, ((1,), (0,)))


def mm_t(a, b):
    return dot(a, b, ((1,), (1,)))


def t_mm(a, b):
    return dot(a, b, ((0,), (0,)))


def build(n_e, n_w):
    bits = [1 << b for b in range(n_e.bit_length() - 1)]
    plane = bits[1:]
    nd = len(plane)

    def swap(x, d):
        return lax.ppermute(x, "expert", [(i, i ^ d) for i in range(n_e)])

    def shift(x, s):
        return lax.ppermute(x, "wshard", [(j, (j + s) % n_w) for j in range(n_w)])

    def joint(x, pairs):
        return lax.ppermute(x, AXES, pairs)

    def line_gather(x):
        return [x] + [shift(x, n_w - r) for r in range(1, n_w)]

    def line_scatter(blocks):
        total = blocks[0].astype(F32)
        for r in range(1, n_w):
            total = total + shift(blocks[r], r).astype(F32)
        return total

    def line_exchange(x, shard):
        out = jnp.zeros_like(x)
        for s in range(n_w):
            got = lax.dynamic_index_in_dim(x, (shard + s) % n_w, 0, keepdims=False)
            got = shift(got, s) if s else got
            out = lax.dynamic_update_index_in_dim(out, got, (shard - s + n_w) % n_w, 0)
        return out

    def line_sum(x, shard):
        x = jnp.roll(x.reshape(2, n_w, -1), shard, axis=1)
        return jnp.roll(lax.psum(x, "wshard"), -shard, axis=1)

    def plane_gather(parts):
        held = [([0], x) for x in parts]
        groups = [held]
        for step in range(nd):
            got = []
            for p, (masks, x) in enumerate(held):
                d = plane[(step + p) % nd]
                got.append(([m | d for m in masks], swap(x, d)))
            groups.append(got)
            held = [
                (a[0] + b[0], jnp.concatenate([a[1], b[1]], 0)) if step + 1 < nd else None
                for a, b in zip(held, got)
            ]
        return groups

    def plane_scatter(groups):
        out = []
        for p in range(nd):
            mine = [groups[step][p] for step in range(nd + 1)]
            for step in reversed(range(nd)):
                got = swap(mine[step + 1], plane[(step + p) % nd])
                at = 0
                for low in range(step + 1):
                    n = mine[low].shape[0]
                    mine[low] = (mine[low].astype(F32) + got[at : at + n].astype(F32)).astype(LOW)
                    at += n
            out.append(mine[0])
        return out

    def hyper_scatter(x, me, dims, kind):
        x = x.reshape((2,) * len(bits) + x.shape[1:])
        left = list(reversed(bits))
        for d in dims:
            at = left.index(d)
            bit = (me // d) % 2
            send = lax.dynamic_index_in_dim(x, 1 - bit, at, keepdims=False).astype(kind)
            keep = lax.dynamic_index_in_dim(x, bit, at, keepdims=False)
            x = (keep.astype(F32) + swap(send, d).astype(F32)).astype(kind)
            left.pop(at)
        return x

    def local(
        hidden_in,
        doc_ids,
        routes,
        attn_gain,
        q_gain,
        k_gain,
        ffn_gain,
        w_qkv,
        w_out,
        w_router,
        w_gate_up,
        w_down,
        cotangent,
    ):
        micro = hidden_in.shape[0]
        rows = hidden_in.shape[2]
        width = hidden_in.shape[3]
        heads = HEADS
        head = width // heads
        my_heads = heads // n_w
        cols = width // n_w
        experts = w_router.shape[1]
        local_experts = w_gate_up.shape[0]
        units = w_down.shape[1]
        own = micro * rows
        seq = n_w * rows
        me = lax.axis_index("expert")
        shard = lax.axis_index("wshard")
        scale = head ** (-0.5)

        tokens = hidden_in.reshape(own, width).astype(F32)
        scale_one = rms_scale(tokens)
        normed = (tokens * scale_one * attn_gain).astype(LOW)
        normed_all = jnp.concatenate(line_gather(normed), 0)

        piece = width // n_w // n_e
        mine = lax.dynamic_slice_in_dim(w_qkv, me * piece, piece, 0)
        mine = mine.reshape(piece, 3, n_w, cols).transpose(2, 0, 1, 3).reshape(n_w, piece, 3 * cols)
        bank = line_exchange(mine, shard)
        w_heads = jnp.zeros((n_e, n_w, piece, 3 * cols), LOW)
        half = piece // 2
        for p in range(2):
            masks, held = [0], bank[None, :, p * half : (p + 1) * half]
            for d in plane[p:] + plane[:p] + [1]:
                masks = masks + [m | d for m in masks]
                held = jnp.concatenate([held, swap(held, d)], 0)
            for at, m in enumerate(masks):
                w_heads = lax.dynamic_update_slice(
                    w_heads, held[at : at + 1], (jnp.bitwise_xor(me, m), 0, p * half, 0)
                )
        w_heads = w_heads.transpose(1, 0, 2, 3).reshape(width, 3 * cols)

        used = jnp.any(
            routes.reshape(own, -1, 1) == jnp.arange(experts, dtype=jnp.int32), axis=1
        ).astype(LOW)
        small = jnp.concatenate([w_router.reshape(-1, 128), used.reshape(-1, 128)], 0)
        cut = w_router.size // 128
        small = jnp.stack(line_gather(small))
        router = jnp.roll(small[:, :cut], shard, axis=0).reshape(width, experts)
        used = small[:, cut:].reshape(n_w, own, experts)

        hidden = units * local_experts // n_w
        up = w_gate_up.reshape(local_experts, -1, 2, n_w // local_experts, hidden)
        up = up.transpose(0, 3, 1, 2, 4).reshape(n_w, -1, 2 * hidden)
        dn = w_down.reshape(n_w, hidden, cols)
        up, dn, normed_all = lax.optimization_barrier((up, dn, normed_all))
        up = line_exchange(up, shard).reshape(width, 2 * hidden)
        dn = line_exchange(dn, shard).transpose(1, 0, 2).reshape(hidden, width)
        w_up = [up, swap(up, 1)]
        w_dn = [dn, swap(dn, 1)]
        my_expert = local_experts * me + shard * local_experts // n_w
        sib_expert = local_experts * jnp.bitwise_xor(me, 1) + shard * local_experts // n_w

        projected = mm(normed_all, w_heads)
        raw = projected.reshape(n_w, micro, rows, 3, my_heads, head)
        squares = jnp.sum(projected.reshape(-1, 3, cols)[:, :2] ** 2, axis=-1).T
        scales = lax.rsqrt(line_sum(squares, shard) / width + EPS)
        scales = scales.reshape(2, n_w, micro, rows, 1, 1)
        gain_q = lax.dynamic_slice_in_dim(q_gain, shard * cols, cols).reshape(my_heads, head)
        gain_k = lax.dynamic_slice_in_dim(k_gain, shard * cols, cols).reshape(my_heads, head)
        block_at = (shard + jnp.arange(n_w, dtype=jnp.int32)) % n_w
        positions = (
            block_at[:, None] * rows + jnp.arange(rows, dtype=jnp.int32)[None, :]
        )
        freq = THETA ** (-(jnp.arange(head // 2, dtype=F32) * 2.0 / head))
        angle = positions.astype(F32)[:, None, :, None, None] * freq
        cosine, sine = jnp.cos(angle), jnp.sin(angle)
        q_raw, k_raw, v_raw = raw[..., 0, :, :], raw[..., 1, :, :], raw[..., 2, :, :]
        queries = rotate(q_raw * scales[0] * gain_q, cosine, sine).astype(LOW)
        keys = rotate(k_raw * scales[1] * gain_k, cosine, sine).astype(LOW)
        values = v_raw.astype(LOW)

        def by_head(x):
            return x.transpose(1, 3, 0, 2, 4).reshape(micro * my_heads, seq, head)

        def by_token(x):
            x = x.reshape(micro, my_heads, n_w, rows, head)
            return x.transpose(2, 0, 3, 1, 4)

        q_h, k_h, v_h = by_head(queries), by_head(keys), by_head(values)
        flat_pos = positions.reshape(seq)
        docs = jnp.take(doc_ids[:, 0], flat_pos, axis=1)
        allowed = (flat_pos[None, :] <= flat_pos[:, None])[None] & (
            docs[:, :, None] == docs[:, None, :]
        )
        allowed = jnp.repeat(allowed, my_heads, axis=0)
        scores = jnp.einsum("bqd,bkd->bqk", q_h, k_h, preferred_element_type=F32) * scale
        scores = jnp.where(allowed, scores, -1e30)
        peak = jnp.max(scores, axis=-1, keepdims=True)
        expo = jnp.exp(scores - peak)
        probs = expo / jnp.sum(expo, axis=-1, keepdims=True)
        probs_low = probs.astype(LOW)
        attended = jnp.einsum("bqk,bkd->bqd", probs_low, v_h, preferred_element_type=F32)
        attended = by_token(attended.astype(LOW)).reshape(n_w * own, cols)
        branch = mm(attended, w_out).astype(LOW).reshape(n_w, own, width)
        resid = tokens + line_scatter([branch[r] for r in range(n_w)])

        scale_two = rms_scale(resid)
        ffn_in = (resid * scale_two * ffn_gain).astype(LOW)
        upstream = cotangent.reshape(own, width)
        per = n_w // nd
        expert_at = jnp.arange(experts, dtype=jnp.int32)[None, :]
        hots = [(expert_at == e).astype(F32) for e in (my_expert, sib_expert)]

        def to_parts(blocks):
            return [jnp.concatenate(blocks[p * per : (p + 1) * per], 0) for p in range(nd)]

        def to_owner(groups):
            blocks = []
            for part in plane_scatter(groups):
                blocks += jnp.split(part, per, 0)
            return line_scatter(blocks)

        def run_experts(ffn_rows, dy_rows, used_rows, grads):
            grad_up, grad_dn, grad_router = grads
            used = plane_gather(to_parts(used_rows))
            dy_groups = plane_gather(to_parts(line_gather(dy_rows)))
            x_groups = plane_gather(to_parts(line_gather(ffn_rows)))
            mix_parts, back_parts = [], []
            for x_group, dy_group, used_group in zip(x_groups, dy_groups, used):
                x = jnp.concatenate([b for _, b in x_group], 0)
                dy = jnp.concatenate([b for _, b in dy_group], 0)
                mask = jnp.concatenate([b for _, b in used_group], 0).astype(F32)
                gate_all = jax.nn.softmax(mm(x, router), axis=-1)
                mix, back, dlogits = 0.0, 0.0, 0.0
                for h in range(2):
                    gate = jnp.sum(gate_all * mask * hots[h], axis=-1, keepdims=True)
                    gate_up = mm(x, w_up[h])
                    g, u = gate_up[:, :hidden], gate_up[:, hidden:]
                    sigma = jax.nn.sigmoid(g)
                    silu = g * sigma
                    act = (silu * u).astype(LOW).astype(F32)
                    lifted = mm_t(dy, w_dn[h])
                    dgate = jnp.sum(act * lifted, axis=-1, keepdims=True)
                    act_gated = (act * gate).astype(LOW)
                    dact = lifted * gate
                    dgu = jnp.concatenate(
                        [dact * u * (sigma * (1.0 + g * (1.0 - sigma))), dact * silu], axis=-1
                    ).astype(LOW)
                    dlogits = dlogits + dgate * gate * (hots[h] - gate_all)
                    mix = mix + mm(act_gated, w_dn[h])
                    back = back + mm_t(dgu, w_up[h])
                    grad_up[h] = grad_up[h] + t_mm(x, dgu)
                    grad_dn[h] = grad_dn[h] + t_mm(act_gated, dy)
                dlogits = dlogits.astype(LOW)
                back = (back + mm_t(dlogits, router)).astype(LOW)
                grad_router = grad_router + t_mm(x, dlogits)
                mix_parts.append(jnp.split(mix.astype(LOW), nd, 0))
                back_parts.append(jnp.split(back, nd, 0))
            return to_owner(back_parts), to_owner(mix_parts), (grad_up, grad_dn, grad_router)

        rounds = max(1, n_e * n_w * own // 2 // ROUND_TOKENS)
        step = own // rounds
        grads = ([0.0, 0.0], [0.0, 0.0], 0.0)
        dffn, mixture = [], []
        for n in range(rounds):
            at = n * step
            ffn_rows, dy_rows = ffn_in[at : at + step], upstream[at : at + step]
            if n:
                ffn_rows, dy_rows, grads, dffn, mixture = lax.optimization_barrier(
                    (ffn_rows, dy_rows, grads, dffn, mixture)
                )
            used_rows = [used[r, at : at + step] for r in range(n_w)]
            back, mix, grads = run_experts(ffn_rows, dy_rows, used_rows, grads)
            dffn.append(back)
            mixture.append(mix)
        dffn, mixture = jnp.concatenate(dffn, 0), jnp.concatenate(mixture, 0)
        grad_up, grad_dn, grad_router = grads
        hidden_out = (resid + mixture).astype(LOW)

        up_sum = (grad_up[0] + swap(grad_up[1].astype(LOW), 1).astype(F32)).astype(LOW)
        dn_sum = (grad_dn[0] + swap(grad_dn[1].astype(LOW), 1).astype(F32)).astype(LOW)
        up_sum = line_exchange(up_sum.reshape(n_w, cols, 2 * hidden), shard)
        dn_sum = dn_sum.reshape(hidden, n_w, cols).transpose(1, 0, 2)
        dn_sum = line_exchange(dn_sum, shard)
        up_sum = up_sum.reshape(local_experts, n_w // local_experts, cols, 2, hidden)
        out_gate_up = up_sum.transpose(0, 2, 3, 1, 4).reshape(w_gate_up.shape).astype(F32)
        out_down = dn_sum.reshape(w_down.shape).astype(F32)

        upstream = upstream.astype(F32)
        weighted = ffn_gain * dffn
        inner = jnp.mean(resid * weighted, axis=-1, keepdims=True)
        dresid = upstream + norm_back(resid, scale_two, ffn_gain, dffn, inner)
        grad_ffn_gain = jnp.sum(dffn * resid * scale_two, axis=0)
        dbranch = jnp.concatenate(line_gather(dresid.astype(LOW)), 0)
        grad_out = t_mm(attended, dbranch)
        dattended = mm_t(dbranch, w_out).astype(LOW)
        datt_h = by_head(dattended.reshape(n_w, micro, rows, my_heads, head))
        dprobs = jnp.einsum("bqd,bkd->bqk", datt_h, v_h, preferred_element_type=F32)
        probs = jnp.where(allowed, probs, 0.0)
        dscores = probs * (dprobs - jnp.sum(probs * dprobs, axis=-1, keepdims=True))
        dscores = dscores.astype(LOW)
        dq = jnp.einsum("bqk,bkd->bqd", dscores, k_h, preferred_element_type=F32) * scale
        dk = jnp.einsum("bqk,bqd->bkd", dscores, q_h, preferred_element_type=F32) * scale
        dv = jnp.einsum("bqk,bqd->bkd", probs_low, datt_h, preferred_element_type=F32)
        dq = rotate(by_token(dq), cosine, -sine)
        dk = rotate(by_token(dk), cosine, -sine)
        dv = by_token(dv)
        inners = jnp.stack(
            [
                jnp.sum(q_raw * gain_q * dq, axis=(-2, -1)),
                jnp.sum(k_raw * gain_k * dk, axis=(-2, -1)),
            ]
        )
        inners = line_sum(inners, shard) / width
        inners = inners.reshape(2, n_w, micro, rows, 1, 1)
        dq_raw = norm_back(q_raw, scales[0], gain_q, dq, inners[0])
        dk_raw = norm_back(k_raw, scales[1], gain_k, dk, inners[1])
        grad_q = jnp.sum(dq * q_raw * scales[0], axis=(0, 1, 2)).reshape(cols)
        grad_k = jnp.sum(dk * k_raw * scales[1], axis=(0, 1, 2)).reshape(cols)
        dproj = jnp.stack([dq_raw, dk_raw, dv], axis=3).astype(LOW)
        dproj = dproj.reshape(n_w * own, 3 * cols)
        dnormed = mm_t(dproj, w_heads).astype(LOW).reshape(n_w, own, width)
        dnormed = line_scatter([dnormed[r] for r in range(n_w)])
        inner = jnp.mean(tokens * (attn_gain * dnormed), axis=-1, keepdims=True)
        dx = norm_back(tokens, scale_one, attn_gain, dnormed, inner)
        grad_in = (dresid + dx).astype(LOW)
        grad_attn_gain = jnp.sum(dnormed * tokens * scale_one, axis=0)
        grad_qkv = t_mm(normed_all, dproj)

        small = width // (n_e * n_w)
        core_first = [1] + plane
        qkv = hyper_scatter(grad_qkv.reshape(n_e, n_w * small, 3 * cols), me, core_first, LOW)
        qkv = line_exchange(qkv.reshape(n_w, small, 3 * cols), shard)
        qkv = qkv.reshape(n_w, small, 3, cols).transpose(1, 2, 0, 3)
        out_qkv = qkv.reshape(small, 3 * width).astype(F32)
        to_rows = [
            (i * n_w + w, w * n_e + i) for i in range(n_e) for w in range(n_w)
        ]
        out_rows = hyper_scatter(grad_out.reshape(n_e, small, width), me, core_first, LOW)
        out_rows = joint(out_rows, to_rows).astype(F32)
        gains = jnp.stack([grad_q, grad_k]).reshape(2, n_e, small).transpose(1, 0, 2)
        gains = joint(hyper_scatter(gains, me, core_first, F32), to_rows)
        pack = jnp.concatenate([grad_router.T, grad_attn_gain[None], grad_ffn_gain[None]], 0)
        pack = pack.reshape(experts + 2, n_e, n_w * small).transpose(1, 0, 2)
        pack = hyper_scatter(pack, me, core_first, F32)
        pack = pack.reshape(experts + 2, n_w, small)
        total = 0.0
        for s in range(n_w):
            got = lax.dynamic_index_in_dim(pack, (shard + s) % n_w, 1, keepdims=False)
            total = total + (shift(got, s) if s else got)
        return (
            hidden_out.reshape(micro, 1, rows, width),
            grad_in.reshape(micro, 1, rows, width),
            total[experts],
            gains[0],
            gains[1],
            total[experts + 1],
            out_qkv,
            out_rows,
            total[:experts].T,
            out_gate_up,
            out_down,
        )

    return local


def solution(mesh):
    in_specs = (
        P(None, "expert", "wshard", None),
        P(None, "expert", None),
        P(None, "expert", "wshard", None),
        P(),
        P(),
        P(),
        P(),
        P("wshard", None),
        P("wshard", None),
        P("wshard", None),
        P("expert", "wshard", None),
        P("expert", None, "wshard"),
        P(None, "expert", "wshard", None),
    )
    out_specs = (
        P(None, "expert", "wshard", None),
        P(None, "expert", "wshard", None),
        P(("expert", "wshard")),
        P(("expert", "wshard")),
        P(("expert", "wshard")),
        P(("expert", "wshard")),
        P(("expert", "wshard"), None),
        P(("expert", "wshard"), None),
        P(("expert", "wshard"), None),
        P("expert", "wshard", None),
        P("expert", None, "wshard"),
    )
    local = build(mesh.shape["expert"], mesh.shape["wshard"])
    return jax.shard_map(local, mesh=mesh, in_specs=in_specs, out_specs=out_specs, check_vma=False)
```

```python
import functools

import jax
import jax.numpy as jnp
from jax import lax
from jax.experimental import pallas as pl
from jax.experimental.pallas import tpu as pltpu
from jax.sharding import PartitionSpec as P

HEADS = 16
EPS = 1e-05
THETA = 10000.0
ROUND_TOKENS = 2048
AXES = ("expert", "wshard")
LOW = jnp.bfloat16
F32 = jnp.float32


def rms_scale(values):
    return lax.rsqrt(jnp.mean(values * values, axis=-1, keepdims=True) + EPS)


def norm_back(values, scale, gain, grads, inner):
    weighted = gain * grads
    return scale * weighted - values * scale * scale * scale * inner


def dot(a, b, dims):
    return lax.dot_general(a, b, (dims, ((), ())), preferred_element_type=F32)


def mm(a, b):
    return dot(a, b, ((1,), (0,)))


def mm_t(a, b):
    return dot(a, b, ((1,), (1,)))


def t_mm(a, b):
    return dot(a, b, ((0,), (0,)))


def tie(x, *after):
    return lax.optimization_barrier((x, after))[0]


LIGHT = pl.CostEstimate(flops=1, bytes_accessed=1, transcendentals=0)


def turned(x, cos_ref, sin_ref, sign):
    return x * cos_ref[...] + sign * pltpu.roll(x, x.shape[1] // 2, 1) * sin_ref[...]


def attention_parts(q_ref, k_ref, v_ref, scale_ref, gain_ref, cos_ref, sin_ref, mask_ref):
    seq, head = cos_ref.shape
    raw_q = q_ref[:, 0].reshape(seq, head)
    raw_k = k_ref[:, 0].reshape(seq, head)
    values = v_ref[:, 0].reshape(seq, head).astype(LOW)
    scales = scale_ref[:, 0].reshape(seq, 2)
    hat_q = raw_q * scales[:, 0:1] * gain_ref[0:1, :]
    hat_k = raw_k * scales[:, 1:2] * gain_ref[1:2, :]
    queries = turned(hat_q, cos_ref, sin_ref, 1.0).astype(LOW)
    keys = turned(hat_k, cos_ref, sin_ref, 1.0).astype(LOW)
    scores = mm_t(queries, keys) * head ** (-0.5)
    scores = jnp.where(mask_ref[0] > 0, scores, -1e30)
    expo = jnp.exp(scores - jnp.max(scores, axis=-1, keepdims=True))
    probs = expo / jnp.sum(expo, axis=-1, keepdims=True)
    return raw_q, raw_k, values, scales, queries, keys, probs


def attention_kernel(*refs):
    out_ref = refs[-1]
    _, _, values, _, _, _, probs = attention_parts(*refs[:-1])
    out = mm(probs.astype(LOW), values).astype(LOW)
    out_ref[...] = out.reshape(out_ref.shape)


def attention_back_kernel(*refs):
    grad_ref, (dq_ref, dk_ref, dv_ref, inner_ref, gains_ref) = refs[8], refs[9:]
    gain_ref, cos_ref, sin_ref = refs[4:7]
    raw_q, raw_k, values, scales, queries, keys, probs = attention_parts(*refs[:8])
    seq, head = cos_ref.shape
    grad = grad_ref[:, 0].reshape(seq, head)
    dprobs = mm_t(grad, values)
    dscores = probs * (dprobs - jnp.sum(probs * dprobs, axis=-1, keepdims=True))
    dscores = dscores.astype(LOW)
    dq = turned(mm(dscores, keys) * head ** (-0.5), cos_ref, sin_ref, -1.0)
    dk = turned(t_mm(dscores, queries) * head ** (-0.5), cos_ref, sin_ref, -1.0)
    dv = t_mm(probs.astype(LOW), grad)
    dq_ref[...] = dq.reshape(dq_ref.shape)
    dk_ref[...] = dk.reshape(dk_ref.shape)
    dv_ref[...] = dv.astype(LOW).reshape(dv_ref.shape)
    inner_q = jnp.sum(raw_q * gain_ref[0:1, :] * dq, axis=-1, keepdims=True)
    inner_k = jnp.sum(raw_k * gain_ref[1:2, :] * dk, axis=-1, keepdims=True)
    inner_ref[...] = jnp.concatenate([inner_q, inner_k], 1).reshape(inner_ref.shape)
    gains_ref[0, 0:1, :] = jnp.sum(dq * raw_q * scales[:, 0:1], axis=0, keepdims=True)
    gains_ref[0, 1:2, :] = jnp.sum(dk * raw_k * scales[:, 1:2], axis=0, keepdims=True)


def attention_call(projected, scales, gains, cosine, sine, mask, grad=None):
    n_w, micro, rows, cols = projected.shape
    seq, head = cosine.shape
    cols = cols // 3
    heads = cols // head

    def part(p):
        return pl.BlockSpec((n_w, 1, rows, head), lambda m, h: (0, m, 0, p * heads + h))

    fixed = pl.BlockSpec((seq, head), lambda m, h: (0, 0))
    specs = [part(0), part(1), part(2)]
    specs.append(pl.BlockSpec((n_w, 1, rows, 2), lambda m, h: (0, m, 0, 0)))
    specs.append(pl.BlockSpec((2, head), lambda m, h: (0, h)))
    specs += [fixed, fixed, pl.BlockSpec((1, seq, seq), lambda m, h: (m, 0, 0))]
    ins = [projected] * 3 + [scales, gains, cosine, sine, mask]

    def like(kind):
        return jax.ShapeDtypeStruct((n_w, micro, rows, cols), kind)

    if grad is None:
        kernel, outs, out_specs = attention_kernel, like(LOW), part(0)
    else:
        ins, specs = ins + [grad], specs + [part(0)]
        kernel = attention_back_kernel
        outs = [
            like(F32),
            like(F32),
            like(LOW),
            jax.ShapeDtypeStruct((heads, n_w, micro, rows, 2), F32),
            jax.ShapeDtypeStruct((micro, 2, cols), F32),
        ]
        out_specs = [part(0)] * 3 + [
            pl.BlockSpec((1, n_w, 1, rows, 2), lambda m, h: (h, 0, m, 0, 0)),
            pl.BlockSpec((1, 2, head), lambda m, h: (m, 0, h)),
        ]
    return pl.pallas_call(
        kernel,
        grid=(micro, heads),
        in_specs=specs,
        out_specs=out_specs,
        out_shape=outs,
        compiler_params=pltpu.CompilerParams(vmem_limit_bytes=32 * 1024 * 1024),
        cost_estimate=LIGHT,
        name="attention" if grad is None else "attention_back",
    )(*ins)


def pack_kernel(at_ref, up_ref, down_ref, out_ref):
    step = pl.program_id(0)

    @pl.when(step < 2)
    def _():
        out_ref[...] = up_ref[0]

    @pl.when(step == 2)
    def _():
        out_ref[...] = down_ref[0]


def pack_half(t, w_gate_up, w_down, halves):
    rows = w_gate_up.shape[1]
    hidden = w_down.shape[1] // halves
    cols = w_down.shape[2]

    def up_at(i, at):
        return (at[0] // halves, 0, jnp.minimum(i, 1) * halves + at[0] % halves)

    def down_at(i, at):
        return (at[0] // halves, at[0] % halves, 0)

    return pl.pallas_call(
        pack_kernel,
        grid_spec=pltpu.PrefetchScalarGridSpec(
            num_scalar_prefetch=1,
            grid=(3,),
            in_specs=[
                pl.BlockSpec((1, rows, hidden), up_at),
                pl.BlockSpec((1, hidden, cols), down_at),
            ],
            out_specs=pl.BlockSpec((rows, hidden), lambda i, at: (0, i)),
        ),
        out_shape=jax.ShapeDtypeStruct((rows, 3 * hidden), LOW),
        name="pack",
    )(t.reshape(1), w_gate_up, w_down)


def unpack_kernel(n_w, shard_ref, *refs):
    pieces, (up_ref, down_ref) = refs[:n_w], refs[n_w:]
    halves, hidden = down_ref.shape[1], pieces[0].shape[1] // 3
    units = halves * hidden
    for s in range(n_w):
        t = lax.rem(shard_ref[0] - s + n_w, n_w)
        j, h = lax.div(t, halves), lax.rem(t, halves)
        for part in range(2):
            at = pl.multiple_of(part * units + h * hidden, 128)
            piece = pieces[s][:, part * hidden : (part + 1) * hidden]
            up_ref[j, :, pl.ds(at, hidden)] = piece.astype(F32)
        down_ref[j, h] = pieces[s][:, 2 * hidden :].astype(F32)


def unpack(pieces, shard, experts):
    n_w = len(pieces)
    rows, hidden = pieces[0].shape[0], pieces[0].shape[1] // 3
    halves = n_w // experts
    cols = hidden
    tile = min(128, rows)
    up, down = pl.pallas_call(
        functools.partial(unpack_kernel, n_w),
        grid_spec=pltpu.PrefetchScalarGridSpec(
            num_scalar_prefetch=1,
            grid=(rows // tile,),
            in_specs=[pl.BlockSpec((tile, 3 * hidden), lambda i, at: (i, 0))] * n_w,
            out_specs=[
                pl.BlockSpec((experts, tile, 2 * halves * hidden), lambda i, at: (0, i, 0)),
                pl.BlockSpec((experts, halves, tile, cols), lambda i, at: (0, 0, i, 0)),
            ],
        ),
        out_shape=[
            jax.ShapeDtypeStruct((experts, rows, 2 * halves * hidden), F32),
            jax.ShapeDtypeStruct((experts, halves, hidden, cols), F32),
        ],
        compiler_params=pltpu.CompilerParams(vmem_limit_bytes=32 * 1024 * 1024),
        name="unpack",
    )(shard.reshape(1), *pieces)
    return up, down.reshape(experts, halves * hidden, cols)


def expert_kernel(experts, n_w, at_ref, place_ref, x_ref, dy_all_ref, used_ref, hot_ref, *refs):
    router_ref, back_router_ref, refs = refs[0], refs[1], refs[2:]
    packs, refs = (refs[:n_w], refs[n_w : 2 * n_w]), refs[2 * n_w :]
    mix_ref, back_ref, dy_ref, dlogits_ref = refs[:4]
    dgu_refs, gated_refs = refs[4:6], refs[6:8]
    dy_ref[...] = dy_all_ref[...].reshape(dy_ref.shape)
    hidden = packs[0][0].shape[1] // 3
    cols = packs[0][0].shape[0]
    spans = [pl.ds(pl.multiple_of(at_ref[s] * cols, 128), cols) for s in range(n_w)]
    lane = lax.broadcasted_iota(jnp.int32, (1, router_ref.shape[1]), 1)
    logits = jnp.where(lane < experts, mm(x_ref[...], router_ref[...]), -1e30)
    expo = jnp.exp(logits - jnp.max(logits, axis=-1, keepdims=True))
    gate_all = expo / jnp.sum(expo, axis=-1, keepdims=True)
    used = gate_all * used_ref[...].astype(F32)
    dlogits = jnp.zeros_like(gate_all)
    for h in range(2):
        hot = hot_ref[h : h + 1, :]
        gate = jnp.sum(used * hot, axis=-1, keepdims=True)
        g = u = lifted = 0.0
        for s in range(n_w):
            g = g + mm(x_ref[:, spans[s]], packs[h][s][:, :hidden])
            u = u + mm(x_ref[:, spans[s]], packs[h][s][:, hidden : 2 * hidden])
            lifted = lifted + mm_t(dy_ref[:, spans[s]], packs[h][s][:, 2 * hidden :])
        sigma = jax.nn.sigmoid(g)
        silu = g * sigma
        act = (silu * u).astype(LOW).astype(F32)
        dgate = jnp.sum(act * lifted, axis=-1, keepdims=True)
        gated_refs[h][...] = (act * gate).astype(LOW)
        dact = lifted * gate
        dgu_refs[h][:, :hidden] = (dact * u * (sigma * (1.0 + g * (1.0 - sigma)))).astype(LOW)
        dgu_refs[h][:, hidden:] = (dact * silu).astype(LOW)
        dlogits = dlogits + dgate * gate * (hot - gate_all)
    dlogits = dlogits.astype(LOW)
    dlogits_ref[...] = dlogits
    for s in range(n_w):
        back = mm_t(dgu_refs[0][...], packs[0][s][:, : 2 * hidden])
        back = back + mm_t(dgu_refs[1][...], packs[1][s][:, : 2 * hidden])
        back = back + mm(dlogits, back_router_ref[:, spans[s]])
        back_ref[:, spans[s]] = back.astype(LOW)
    for s in range(n_w):
        mix = mm(gated_refs[0][...], packs[0][s][:, 2 * hidden :])
        mix = mix + mm(gated_refs[1][...], packs[1][s][:, 2 * hidden :])
        mix_ref[:, spans[s]] = mix.astype(LOW)


def expert_pass(x, dy, rows, used, hots, router, packs, at, place, experts):
    n, width = x.shape
    n_w = len(packs[0])
    tile = 2 * rows
    cols, hidden = packs[0][0].shape[0], packs[0][0].shape[1] // 3
    lanes = used.shape[1]

    def tiled(cols):
        return pl.BlockSpec((tile, cols), lambda i, at, place: (i, 0))

    def placed(cols):
        return pl.BlockSpec((tile, cols), lambda i, at, place: (place[i], 0))

    def fixed(shape):
        return pl.BlockSpec(shape, lambda i, at, place: (0, 0), pipeline_mode=pl.Buffered(1))

    router = jnp.pad(router, ((0, 0), (0, lanes - experts)))
    outs = [width, width, width, lanes, 2 * hidden, 2 * hidden, hidden, hidden]
    return pl.pallas_call(
        functools.partial(expert_kernel, experts, n_w),
        grid_spec=pltpu.PrefetchScalarGridSpec(
            num_scalar_prefetch=2,
            grid=(n // tile,),
            in_specs=[
                tiled(width),
                pl.BlockSpec((2, rows, width), lambda i, at, place: (place[i], 0, 0)),
                placed(lanes),
            ]
            + [fixed((2, lanes)), fixed((width, lanes)), fixed((lanes, width))]
            + [fixed((cols, 3 * hidden))] * (2 * n_w),
            out_specs=[placed(width)] + [tiled(c) for c in outs[1:]],
        ),
        out_shape=[jax.ShapeDtypeStruct((n, c), LOW) for c in outs],
        compiler_params=pltpu.CompilerParams(vmem_limit_bytes=56 * 1024 * 1024),
        cost_estimate=LIGHT,
        name="expert_pass",
    )(at, place, x, dy, used, hots, router, router.T, *packs[0], *packs[1])


def grad_kernel(shard_ref, x_ref, dy_ref, dgu_ref, gated_ref, *refs):
    out_ref = refs[-1]
    hidden = gated_ref.shape[1]
    if len(refs) > 1:
        dlogits_ref, out_ref, router_ref = refs
        router_ref[...] = t_mm(x_ref[...], dlogits_ref[...])
    out_ref[0, :, : 2 * hidden] = t_mm(x_ref[...], dgu_ref[...]).astype(out_ref.dtype)
    out_ref[0, :, 2 * hidden :] = t_mm(gated_ref[...], dy_ref[...]).astype(out_ref.dtype)


def grad_pass(x, dy, dgu, gated, dlogits, shard, n_w, kind):
    n, width = x.shape
    hidden = gated.shape[1]
    cols = width // n_w

    def fixed(a):
        return pl.BlockSpec(a.shape, lambda i, at: (0, 0), pipeline_mode=pl.Buffered(1))

    column = pl.BlockSpec((n, cols), lambda i, at: (0, lax.rem(at[0] + i, n_w)))
    ins, specs = [x, dy, dgu, gated], [column, column, fixed(dgu), fixed(gated)]
    out_specs = [pl.BlockSpec((1, cols, 3 * hidden), lambda i, at: (i, 0, 0))]
    outs = [jax.ShapeDtypeStruct((n_w, cols, 3 * hidden), kind)]
    if dlogits is not None:
        lanes = dlogits.shape[1]
        ins, specs = ins + [dlogits], specs + [fixed(dlogits)]
        out_specs.append(pl.BlockSpec((cols, lanes), lambda i, at: (lax.rem(at[0] + i, n_w), 0)))
        outs.append(jax.ShapeDtypeStruct((width, lanes), F32))
    return tuple(
        pl.pallas_call(
            grad_kernel,
            grid_spec=pltpu.PrefetchScalarGridSpec(
                num_scalar_prefetch=1, grid=(n_w,), in_specs=specs, out_specs=out_specs
            ),
            out_shape=outs,
            compiler_params=pltpu.CompilerParams(vmem_limit_bytes=56 * 1024 * 1024),
            cost_estimate=LIGHT,
            name="grad_pass",
        )(shard.reshape(1), *ins)
    )


def build(n_e, n_w):
    bits = [1 << b for b in range(n_e.bit_length() - 1)]
    plane = bits[1:]
    nd = len(plane)

    def swap(x, d):
        return lax.ppermute(x, "expert", [(i, i ^ d) for i in range(n_e)])

    def shift(x, s):
        return lax.ppermute(x, "wshard", [(j, (j + s) % n_w) for j in range(n_w)])

    def joint(x, pairs):
        return lax.ppermute(x, AXES, pairs)

    def line_gather(x):
        return [x] + [shift(x, n_w - r) for r in range(1, n_w)]

    def line_scatter(blocks):
        total = blocks[0].astype(F32)
        for r in range(1, n_w):
            total = total + shift(blocks[r], r).astype(F32)
        return total

    def across(x, r):
        return lax.ppermute(x, "wshard", [(j, j ^ r) for j in range(n_w)])

    def pair_parts(x, shard):
        odd = shard % 2 == 1
        blocks = [x] + [across(x, r) for r in range(1, n_w)]
        parts = []
        for a, b in zip(blocks[::2], blocks[1::2]):
            parts.append(jnp.concatenate([jnp.where(odd, b, a), jnp.where(odd, a, b)], 0))
        return parts

    def pair_scatter(parts, shard):
        odd = shard % 2 == 1
        total = 0.0
        for p, part in enumerate(parts):
            a, b = jnp.split(part, 2, 0)
            for r, block in ((2 * p, jnp.where(odd, b, a)), (2 * p + 1, jnp.where(odd, a, b))):
                total = total + (across(block, r) if r else block).astype(F32)
        return total

    def line_exchange(send, shard, order=None):
        got = {0: send(shard)}
        last = None
        for s in order or range(1, n_w):
            x = send((shard + s) % n_w)
            if order and last is not None:
                x = tie(x, last)
            last = got[s] = shift(x, s)
        out = jnp.zeros((n_w,) + got[0].shape, got[0].dtype)
        for s in range(n_w):
            out = lax.dynamic_update_index_in_dim(out, got[s], (shard - s + n_w) % n_w, 0)
        return out

    def line_sum(x, shard):
        x = jnp.roll(x.reshape(2, n_w, -1), shard, axis=1)
        total = x
        for s in range(1, n_w):
            total = total + shift(x, s)
        return jnp.roll(total, -shard, axis=1)

    def way(p, step):
        return plane[(step + p * nd // 2) % nd]

    def plane_gather(parts):
        held = [([0], x) for x in parts]
        groups = [held]
        for step in range(nd):
            got = []
            for p, (masks, x) in enumerate(held):
                got.append(([m | way(p, step) for m in masks], swap(x, way(p, step))))
            groups.append(got)
            held = [
                (a[0] + b[0], jnp.concatenate([a[1], b[1]], 0)) if step + 1 < nd else None
                for a, b in zip(held, got)
            ]
        return groups

    def plane_scatter(groups, beside):
        mine = [[group[p] for group in groups] for p in range(2)]
        for step in reversed(range(nd)):
            got = [swap(mine[p][step + 1], way(p, step)) for p in range(2)]
            if beside is not None:
                got, beside = tie(got, beside), None
            for p in range(2):
                at = 0
                for low in range(step + 1):
                    n = mine[p][low].shape[0]
                    total = mine[p][low].astype(F32) + got[p][at : at + n].astype(F32)
                    mine[p][low] = total.astype(LOW)
                    at += n
            mine = lax.optimization_barrier([m[: step + 1] for m in mine])
        return [m[0] for m in mine]

    def hyper_scatter(x, me, kind, cut=1):
        def halve(x, left, d):
            at = left.index(d)
            bit = (me // d) % 2
            send = lax.dynamic_index_in_dim(x, 1 - bit, at, keepdims=False).astype(kind)
            keep = lax.dynamic_index_in_dim(x, bit, at, keepdims=False)
            return (keep.astype(F32) + swap(send, d).astype(F32)).astype(kind)

        x = x.reshape((2,) * len(bits) + x.shape[1:])
        x = halve(x, list(reversed(bits)), 1)
        parts = []
        for p, part in enumerate(jnp.split(x, cut, -1)):
            left = list(reversed(plane))
            for d in plane[p:] + plane[:p]:
                part = halve(part, left, d)
                left.remove(d)
            parts.append(part)
        return jnp.concatenate(parts, -1)

    def local(
        hidden_in,
        doc_ids,
        routes,
        attn_gain,
        q_gain,
        k_gain,
        ffn_gain,
        w_qkv,
        w_out,
        w_router,
        w_gate_up,
        w_down,
        cotangent,
    ):
        micro = hidden_in.shape[0]
        rows = hidden_in.shape[2]
        width = hidden_in.shape[3]
        heads = HEADS
        head = width // heads
        my_heads = heads // n_w
        cols = width // n_w
        experts = w_router.shape[1]
        local_experts = w_gate_up.shape[0]
        units = w_down.shape[1]
        own = micro * rows
        seq = n_w * rows
        me = lax.axis_index("expert")
        shard = lax.axis_index("wshard")
        scale = head ** (-0.5)

        piece = width // n_w // n_e
        mine = lax.dynamic_slice_in_dim(w_qkv, me * piece, piece, 0)
        mine = mine.reshape(piece, 3, n_w, cols).transpose(2, 0, 1, 3).reshape(n_w, piece, 3 * cols)
        bank = line_exchange(
            lambda t: lax.dynamic_index_in_dim(mine, t, 0, keepdims=False), shard
        )
        upstream = cotangent.reshape(own, width)
        tokens = hidden_in.reshape(own, width).astype(F32)
        scale_one = rms_scale(tokens)
        normed = (tokens * scale_one * attn_gain).astype(LOW)
        used = jnp.any(
            routes.reshape(own, -1, 1) == jnp.arange(experts, dtype=jnp.int32), axis=1
        ).astype(LOW)
        blocks = line_gather(normed)
        blocks, bank = lax.optimization_barrier((blocks, bank))
        normed_all = jnp.concatenate(blocks, 0)

        half = piece // 2
        w_heads = []
        for p in range(2):
            held = bank[:, p * half : (p + 1) * half]
            dims = plane[p:] + plane[:p] + [1]
            for d in dims:
                got, upper = swap(held, d), (me // d) % 2 == 1
                held = jnp.stack([jnp.where(upper, got, held), jnp.where(upper, held, got)])
            at = {d: len(dims) - 1 - k for k, d in enumerate(dims)}
            k = len(dims)
            w_heads.append(held.transpose(k, *[at[d] for d in reversed(bits)], k + 1, k + 2))
        w_heads = jnp.stack(w_heads, 1 + len(bits)).reshape(width, 3 * cols)

        rounds = max(1, n_e * n_w * own // 2 // ROUND_TOKENS)
        step = own // rounds
        hidden = units * local_experts // n_w
        arrived = (shard - jnp.arange(n_w, dtype=jnp.int32) + n_w) % n_w

        def pack_for(t):
            return pack_half(t, w_gate_up, w_down, n_w // local_experts)

        pairs = [
            [(2 * c + k) * n_w + w for c in range(n_e // 2) for w in range(n_w)] for k in range(2)
        ]
        router_rows = w_router.size // width
        used_rows = step * experts // width

        def to_pairs(at):
            rows = [upstream[at : at + step], used[at : at + step].reshape(-1, width)]
            rows.append(w_router.reshape(-1, width))
            rows = jnp.concatenate(rows, 0)
            rows = jnp.pad(rows, ((0, -rows.shape[0] % 16), (0, 0)))
            return lax.all_gather(tie(rows, blocks), AXES, axis_index_groups=pairs)

        dy_all = to_pairs(0)
        pieces = [tie(pack_for((shard + k) % n_w), blocks) for k in range(n_w)]
        pieces = [pieces[k] if k in (0, 2) else shift(pieces[k], k) for k in range(n_w)]

        projected = mm(normed_all, w_heads)
        squares = jnp.sum(projected.reshape(-1, 3, cols)[:, :2] ** 2, axis=-1).T
        scales = lax.rsqrt(line_sum(squares, shard) / width + EPS)
        scales = scales.reshape(2, -1).T
        projected = projected.reshape(n_w, micro, rows, 3 * cols)
        gains = [lax.dynamic_slice_in_dim(g, shard * cols, cols) for g in (q_gain, k_gain)]
        gains = jnp.stack(gains)
        block_at = (shard + jnp.arange(n_w, dtype=jnp.int32)) % n_w
        positions = block_at[:, None] * rows + jnp.arange(rows, dtype=jnp.int32)[None, :]
        positions = positions.reshape(seq)
        freq = THETA ** (-(jnp.arange(head // 2, dtype=F32) * 2.0 / head))
        angle = positions.astype(F32)[:, None] * freq
        cosine, sine = jnp.cos(angle), jnp.sin(angle)
        cosine = jnp.concatenate([cosine, cosine], 1)
        sine = jnp.concatenate([-sine, sine], 1)
        docs = jnp.take(doc_ids[:, 0], positions, axis=1)
        mask = (positions[None, :] <= positions[:, None])[None] & (
            docs[:, :, None] == docs[:, None, :]
        )
        mask = mask.astype(F32)
        attention = functools.partial(
            attention_call,
            projected,
            scales.reshape(n_w, micro, rows, 2),
            gains,
            cosine,
            sine,
            mask,
        )
        attended = attention().reshape(n_w * own, cols)
        branch = mm(attended, w_out).astype(LOW)
        pieces = [p if k in (0, 2) else tie(p, branch) for k, p in enumerate(pieces)]
        branch = branch.reshape(n_w, own, width)
        resid = tokens + line_scatter([branch[r] for r in range(n_w)])

        scale_two = rms_scale(resid)
        ffn_in = (resid * scale_two * ffn_gain).astype(LOW)
        lanes = -(-experts // 128) * 128
        expert_at = jnp.arange(lanes, dtype=jnp.int32)
        my_expert = local_experts * me + shard * local_experts // n_w
        sib_expert = local_experts * jnp.bitwise_xor(me, 1) + shard * local_experts // n_w
        hots = jnp.stack([(expert_at == e).astype(F32) for e in (my_expert, sib_expert)])

        def whole(groups):
            return jnp.concatenate([b for group in groups for _, b in group], 0)

        dffn, mixture = [], []
        grads = None
        for n in range(rounds):
            at = n * step
            ffn_rows = ffn_in[at : at + step]
            if n:
                ffn_rows, grads, dffn, mixture = lax.optimization_barrier(
                    (ffn_rows, grads, dffn, mixture)
                )
                dy_all = to_pairs(at)
            parts = pair_parts(ffn_rows, shard)
            groups = plane_gather(parts)
            x = whole(groups)
            place = [
                jnp.bitwise_xor(me // 2, m // 2) * (n_w // 2) + jnp.bitwise_xor(shard // 2, p)
                for group in groups
                for p in range(2)
                for m in group[p][0]
            ]
            mask = dy_all[:, step : step + used_rows].reshape(-1, experts)
            mask = jnp.pad(mask, ((0, 0), (0, lanes - experts)))
            router = dy_all[:n_w, step + used_rows : step + used_rows + router_rows]
            router = router.reshape(width, experts)
            if n == 0:
                pieces[2] = tie(shift(tie(pieces[2], parts), 2), x)
                siblings = [swap(tie(piece, parts), 1) for piece in pieces]
                packs = [pieces, siblings]
            mix, back, dy, dlogits, dgu0, dgu1, gated0, gated1 = expert_pass(
                x, dy_all, step, mask, hots, router, packs, arrived, jnp.stack(place), experts
            )
            cuts = []
            for group in groups:
                for p in range(2):
                    cuts.append((cuts[-1] if cuts else 0) + group[p][1].shape[0])
            back = jnp.split(back, cuts[:-1], 0)
            back = [back[2 * g : 2 * g + 2] for g in range(nd + 1)]
            kind = LOW if rounds == 1 else F32
            grad_sib, grad_router = grad_pass(x, dy, dgu1, gated1, dlogits, shard, n_w, kind)
            (grad_own,) = grad_pass(x, dy, dgu0, gated0, None, shard, n_w, kind)
            if grads is not None:
                grad_sib, grad_router, grad_own = jax.tree.map(
                    jnp.add, grads, (grad_sib, grad_router, grad_own)
                )
            grads = (grad_sib, grad_router, grad_own)
            beside = grads
            if n == rounds - 1:
                grad_sib = swap(grad_sib.astype(LOW), 1)
                sums = [
                    (grad_own[s].astype(F32) + grad_sib[s].astype(F32)).astype(LOW)
                    for s in range(n_w)
                ]
                beside = sums
            back = plane_scatter(back, beside)
            if n == rounds - 1:
                sums[1], sums[3] = shift(sums[1], 1), shift(sums[3], 3)
                back = tie(back, sums[1])
            dffn.append(pair_scatter(back, shard))
            if n == rounds - 1:
                dffn = tie(dffn, sums[3])
            same = [[2 * c + k for c in range(n_e // 2)] for k in range(2)]
            mixture.append(
                lax.psum_scatter(tie(mix, back), "expert", axis_index_groups=same, tiled=True)
            )
        dffn = jnp.concatenate(dffn, 0)
        grad_router = grad_router[:, :experts]

        upstream = upstream.astype(F32)
        weighted = ffn_gain * dffn
        inner = jnp.mean(resid * weighted, axis=-1, keepdims=True)
        dresid = upstream + norm_back(resid, scale_two, ffn_gain, dffn, inner)
        grad_ffn_gain = jnp.sum(dffn * resid * scale_two, axis=0)
        dbranch = jnp.concatenate(line_gather(dresid.astype(LOW)), 0)
        sums[2] = shift(tie(sums[2], dbranch), 2)
        mixture = [
            lax.psum_scatter(tie(m, dbranch), "wshard", tiled=True).astype(F32) for m in mixture
        ]
        grad_out = t_mm(attended, dbranch)
        dattended = mm_t(dbranch, w_out).astype(LOW)
        dq, dk, dv, inners, grad_gains = attention(dattended.reshape(n_w, micro, rows, cols))
        inners = line_sum(jnp.sum(inners, 0).reshape(-1, 2).T, shard) / width
        inners = inners.reshape(2, -1).T
        flat = projected.reshape(-1, 3 * cols)
        dproj = jnp.concatenate(
            [
                norm_back(
                    flat[:, p * cols : (p + 1) * cols],
                    scales[:, p : p + 1],
                    gains[p],
                    d.reshape(-1, cols),
                    inners[:, p : p + 1],
                ).astype(LOW)
                for p, d in enumerate((dq, dk))
            ]
            + [dv.reshape(-1, cols)],
            1,
        )
        dnormed = tie(mm_t(dproj, w_heads).astype(LOW), sums[2])
        dnormed = dnormed.reshape(n_w, own, width)
        dnormed = line_scatter([dnormed[r] for r in range(n_w)])
        inner = jnp.mean(tokens * (attn_gain * dnormed), axis=-1, keepdims=True)
        dx = norm_back(tokens, scale_one, attn_gain, dnormed, inner)
        grad_in = (dresid + dx).astype(LOW)
        mixture = jnp.concatenate(mixture, 0)
        hidden_out = (resid + mixture).astype(LOW)
        out_gate_up, out_down = unpack(sums, shard, local_experts)
        grad_qkv = t_mm(normed_all, dproj)
        grad_attn_gain = jnp.sum(grad_qkv * w_heads.astype(F32), axis=1) / attn_gain

        small = width // (n_e * n_w)
        qkv = hyper_scatter(grad_qkv.reshape(n_e, n_w * small, 3 * cols), me, LOW, nd)
        qkv_rows = qkv.reshape(n_w, small, 3 * cols)
        qkv = line_exchange(
            lambda t: lax.dynamic_index_in_dim(qkv_rows, t, 0, keepdims=False), shard
        )
        qkv = qkv.reshape(n_w, small, 3, cols).transpose(1, 2, 0, 3)
        out_qkv = qkv.reshape(small, 3 * width).astype(F32)
        to_rows = [
            (i * n_w + w, w * n_e + i) for i in range(n_e) for w in range(n_w)
        ]
        out_rows = hyper_scatter(grad_out.reshape(n_e, small, width), me, LOW)
        out_rows = joint(out_rows, to_rows).astype(F32)
        def all_scatter(x):
            x = x.reshape(-1, n_e, n_w * small).transpose(1, 0, 2)
            x = hyper_scatter(x, me, F32).reshape(-1, n_w, small)
            total = lax.dynamic_index_in_dim(x, shard, 1, keepdims=False)
            for s in range(1, n_w):
                send = lax.dynamic_index_in_dim(x, (shard + s) % n_w, 1, keepdims=False)
                total = total + shift(send, s)
            return total

        gains = jnp.zeros((2, width), F32)
        gains = lax.dynamic_update_slice(gains, jnp.sum(grad_gains, 0), (0, shard * cols))
        pack = [gains, grad_attn_gain[None], grad_ffn_gain[None], grad_router.T]
        pack = all_scatter(jnp.concatenate(pack, 0))
        return (
            hidden_out.reshape(micro, 1, rows, width),
            grad_in.reshape(micro, 1, rows, width),
            pack[2],
            pack[0],
            pack[1],
            pack[3],
            out_qkv,
            out_rows,
            pack[4:].T,
            out_gate_up,
            out_down,
        )

    return local


def solution(mesh):
    in_specs = (
        P(None, "expert", "wshard", None),
        P(None, "expert", None),
        P(None, "expert", "wshard", None),
        P(),
        P(),
        P(),
        P(),
        P("wshard", None),
        P("wshard", None),
        P("wshard", None),
        P("expert", "wshard", None),
        P("expert", None, "wshard"),
        P(None, "expert", "wshard", None),
    )
    out_specs = (
        P(None, "expert", "wshard", None),
        P(None, "expert", "wshard", None),
        P(("expert", "wshard")),
        P(("expert", "wshard")),
        P(("expert", "wshard")),
        P(("expert", "wshard")),
        P(("expert", "wshard"), None),
        P(("expert", "wshard"), None),
        P(("expert", "wshard"), None),
        P("expert", "wshard", None),
        P("expert", None, "wshard"),
    )
    local = build(mesh.shape["expert"], mesh.shape["wshard"])
    return jax.shard_map(local, mesh=mesh, in_specs=in_specs, out_specs=out_specs, check_vma=False)
```

```python
import functools

import jax
import jax.numpy as jnp
from jax import lax
from jax.experimental import pallas as pl
from jax.experimental.pallas import tpu as pltpu
from jax.sharding import PartitionSpec as P

HEADS = 16
EPS = 1e-05
THETA = 10000.0
ROUND_TOKENS = 2048
AXES = ("expert", "wshard")
LOW = jnp.bfloat16
F32 = jnp.float32


def rms_scale(values):
    return lax.rsqrt(jnp.mean(values * values, axis=-1, keepdims=True) + EPS)


def norm_back(values, scale, gain, grads, inner):
    weighted = gain * grads
    return scale * weighted - values * scale * scale * scale * inner


def dot(a, b, dims):
    return lax.dot_general(a, b, (dims, ((), ())), preferred_element_type=F32)


def mm(a, b):
    return dot(a, b, ((1,), (0,)))


def mm_t(a, b):
    return dot(a, b, ((1,), (1,)))


def t_mm(a, b):
    return dot(a, b, ((0,), (0,)))


def both(*arrays):
    return lax.optimization_barrier(arrays)


def tie(x, *after):
    return lax.optimization_barrier((x, after))[0]


def spread_kernel(n_w, shard_ref, *refs):
    out_ref = refs[-1]
    cols = refs[0].shape[1] // 3
    for s in range(n_w):
        t = lax.rem(shard_ref[0] - s + n_w, n_w)
        for part in range(3):
            at = pl.multiple_of((part * n_w + t) * cols, 128)
            out_ref[:, pl.ds(at, cols)] = refs[s][:, part * cols : (part + 1) * cols].astype(F32)


def spread(pieces, shard):
    n_w = len(pieces)
    rows, width = pieces[0].shape
    return pl.pallas_call(
        functools.partial(spread_kernel, n_w),
        grid_spec=pltpu.PrefetchScalarGridSpec(
            num_scalar_prefetch=1,
            grid=(1,),
            in_specs=[pl.BlockSpec((rows, width), lambda i, at: (0, 0))] * n_w,
            out_specs=pl.BlockSpec((rows, n_w * width), lambda i, at: (0, 0)),
        ),
        out_shape=jax.ShapeDtypeStruct((rows, n_w * width), F32),
        name="spread",
    )(shard.reshape(1), *pieces)


LIGHT = pl.CostEstimate(flops=1, bytes_accessed=1, transcendentals=0)


def turned(x, cos_ref, sin_ref, sign):
    return x * cos_ref[...] + sign * pltpu.roll(x, x.shape[1] // 2, 1) * sin_ref[...]


def attention_parts(q_ref, k_ref, v_ref, scale_ref, gain_ref, cos_ref, sin_ref, mask_ref):
    seq, head = cos_ref.shape
    raw_q = q_ref[:, 0].reshape(seq, head)
    raw_k = k_ref[:, 0].reshape(seq, head)
    values = v_ref[:, 0].reshape(seq, head).astype(LOW)
    scales = scale_ref[:, 0].reshape(seq, 2)
    hat_q = raw_q * scales[:, 0:1] * gain_ref[0:1, :]
    hat_k = raw_k * scales[:, 1:2] * gain_ref[1:2, :]
    queries = turned(hat_q, cos_ref, sin_ref, 1.0).astype(LOW)
    keys = turned(hat_k, cos_ref, sin_ref, 1.0).astype(LOW)
    scores = mm_t(queries, keys) * head ** (-0.5)
    scores = jnp.where(mask_ref[0] > 0, scores, -1e30)
    expo = jnp.exp(scores - jnp.max(scores, axis=-1, keepdims=True))
    probs = expo / jnp.sum(expo, axis=-1, keepdims=True)
    return raw_q, raw_k, values, scales, queries, keys, probs


def attention_kernel(*refs):
    out_ref = refs[-1]
    _, _, values, _, _, _, probs = attention_parts(*refs[:-1])
    out = mm(probs.astype(LOW), values).astype(LOW)
    out_ref[...] = out.reshape(out_ref.shape)


def attention_back_kernel(*refs):
    grad_ref, (dq_ref, dk_ref, dv_ref, inner_ref, gains_ref) = refs[8], refs[9:]
    gain_ref, cos_ref, sin_ref = refs[4:7]
    raw_q, raw_k, values, scales, queries, keys, probs = attention_parts(*refs[:8])
    seq, head = cos_ref.shape
    grad = grad_ref[:, 0].reshape(seq, head)
    dprobs = mm_t(grad, values)
    dscores = probs * (dprobs - jnp.sum(probs * dprobs, axis=-1, keepdims=True))
    dscores = dscores.astype(LOW)
    dq = turned(mm(dscores, keys) * head ** (-0.5), cos_ref, sin_ref, -1.0)
    dk = turned(t_mm(dscores, queries) * head ** (-0.5), cos_ref, sin_ref, -1.0)
    dv = t_mm(probs.astype(LOW), grad)
    dq_ref[...] = dq.reshape(dq_ref.shape)
    dk_ref[...] = dk.reshape(dk_ref.shape)
    dv_ref[...] = dv.astype(LOW).reshape(dv_ref.shape)
    inner_q = jnp.sum(raw_q * gain_ref[0:1, :] * dq, axis=-1, keepdims=True)
    inner_k = jnp.sum(raw_k * gain_ref[1:2, :] * dk, axis=-1, keepdims=True)
    inner_ref[...] = jnp.concatenate([inner_q, inner_k], 1).reshape(inner_ref.shape)
    gains_ref[0, 0:1, :] = jnp.sum(dq * raw_q * scales[:, 0:1], axis=0, keepdims=True)
    gains_ref[0, 1:2, :] = jnp.sum(dk * raw_k * scales[:, 1:2], axis=0, keepdims=True)


def attention_call(projected, scales, gains, cosine, sine, mask, grad=None):
    n_w, micro, rows, cols = projected.shape
    seq, head = cosine.shape
    cols = cols // 3
    heads = cols // head

    def part(p):
        return pl.BlockSpec((n_w, 1, rows, head), lambda m, h: (0, m, 0, p * heads + h))

    fixed = pl.BlockSpec((seq, head), lambda m, h: (0, 0))
    specs = [part(0), part(1), part(2)]
    specs.append(pl.BlockSpec((n_w, 1, rows, 2), lambda m, h: (0, m, 0, 0)))
    specs.append(pl.BlockSpec((2, head), lambda m, h: (0, h)))
    specs += [fixed, fixed, pl.BlockSpec((1, seq, seq), lambda m, h: (m, 0, 0))]
    ins = [projected] * 3 + [scales, gains, cosine, sine, mask]

    def like(kind):
        return jax.ShapeDtypeStruct((n_w, micro, rows, cols), kind)

    if grad is None:
        kernel, outs, out_specs = attention_kernel, like(LOW), part(0)
    else:
        ins, specs = ins + [grad], specs + [part(0)]
        kernel = attention_back_kernel
        outs = [
            like(F32),
            like(F32),
            like(LOW),
            jax.ShapeDtypeStruct((heads, n_w, micro, rows, 2), F32),
            jax.ShapeDtypeStruct((micro, 2, cols), F32),
        ]
        out_specs = [part(0)] * 3 + [
            pl.BlockSpec((1, n_w, 1, rows, 2), lambda m, h: (h, 0, m, 0, 0)),
            pl.BlockSpec((1, 2, head), lambda m, h: (m, 0, h)),
        ]
    return pl.pallas_call(
        kernel,
        grid=(micro, heads),
        in_specs=specs,
        out_specs=out_specs,
        out_shape=outs,
        compiler_params=pltpu.CompilerParams(vmem_limit_bytes=32 * 1024 * 1024),
        cost_estimate=LIGHT,
        name="attention" if grad is None else "attention_back",
    )(*ins)


def plane_rows(ref, order):
    picks = range(1 << len(order))
    return jnp.concatenate([ref[tuple((i // d) % 2 for d in order) + (0,)] for i in picks], 0)


def out_kernel(n_w, orders, at_ref, x_ref, gain_ref, *refs):
    pieces, weights, (resid_ref, ffn_ref) = refs[:n_w], refs[n_w : 3 * n_w], refs[3 * n_w :]
    total = []
    for p, order in enumerate(orders):
        half = weights[0].shape[-1]
        part = x_ref[:, p * half : (p + 1) * half].astype(F32)
        for s in range(n_w):
            part = part + mm(pieces[s][...], plane_rows(weights[p * n_w + s], order))
        total.append(part)
    total = jnp.concatenate(total, 1)
    resid_ref[...] = total
    ffn_ref[...] = (total * rms_scale(total) * gain_ref[...]).astype(LOW)


def out_back_kernel(n_w, orders, at_ref, dffn_ref, resid_ref, dy_ref, gain_ref, *refs):
    weights, (dresid_ref, low_ref, sum_ref) = refs[: 2 * n_w], refs[2 * n_w : 2 * n_w + 3]
    outs = refs[2 * n_w + 3 :]
    dffn, resid = dffn_ref[...], resid_ref[...]
    scale = rms_scale(resid)
    weighted = gain_ref[...] * dffn
    inner = jnp.mean(resid * weighted, axis=-1, keepdims=True)
    dresid = dy_ref[...].astype(F32) + norm_back(resid, scale, gain_ref[...], dffn, inner)
    dresid_ref[...] = dresid
    low_ref[...] = dresid.astype(LOW)
    sum_ref[...] = jnp.sum(dffn * resid * scale, axis=0, keepdims=True)
    for s in range(n_w):
        total = 0.0
        for p, order in enumerate(orders):
            half = weights[0].shape[-1]
            weight = plane_rows(weights[p * n_w + s], order)
            total = total + mm_t(low_ref[:, p * half : (p + 1) * half], weight)
        outs[s][...] = total.astype(LOW)


def out_grad_kernel(n_w, orders, at_ref, low_ref, *refs):
    pieces, out_ref = refs[:n_w], refs[n_w]
    cols = pieces[0].shape[1]
    for s in range(n_w):
        rows = pl.ds(pl.multiple_of(at_ref[s] * cols, 128), cols)
        out_ref[rows, :] = t_mm(pieces[s][...], low_ref[...]).astype(LOW)


def out_call(kernel, name, at, ins, weights, orders, outs):
    n_w = at.shape[0]

    def fixed(shape):
        return pl.BlockSpec(shape, lambda i, at: (0,) * len(shape))

    specs = [fixed(a.shape) for a in ins]
    for weight in weights:
        lead = weight.ndim - 3
        shape = weight.shape[:lead] + (1,) + weight.shape[-2:]
        for s in range(n_w):
            specs.append(
                pl.BlockSpec(shape, lambda i, at, s=s, lead=lead: (0,) * lead + (at[s], 0, 0))
            )
        ins = ins + [weight] * n_w
    return pl.pallas_call(
        functools.partial(kernel, n_w, orders),
        grid_spec=pltpu.PrefetchScalarGridSpec(
            num_scalar_prefetch=1,
            grid=(1,),
            in_specs=specs,
            out_specs=[fixed(o.shape) for o in outs],
        ),
        out_shape=outs,
        compiler_params=pltpu.CompilerParams(vmem_limit_bytes=56 * 1024 * 1024),
        cost_estimate=LIGHT,
        name=name,
    )(at, *ins)


def pack_kernel(at_ref, up_ref, down_ref, out_ref):
    step = pl.program_id(0)

    @pl.when(step < 2)
    def _():
        out_ref[...] = up_ref[0]

    @pl.when(step == 2)
    def _():
        out_ref[...] = down_ref[0]


def pack_half(t, w_gate_up, w_down, halves):
    rows = w_gate_up.shape[1]
    hidden = w_down.shape[1] // halves
    cols = w_down.shape[2]

    def up_at(i, at):
        return (at[0] // halves, 0, jnp.minimum(i, 1) * halves + at[0] % halves)

    def down_at(i, at):
        return (at[0] // halves, at[0] % halves, 0)

    return pl.pallas_call(
        pack_kernel,
        grid_spec=pltpu.PrefetchScalarGridSpec(
            num_scalar_prefetch=1,
            grid=(3,),
            in_specs=[
                pl.BlockSpec((1, rows, hidden), up_at),
                pl.BlockSpec((1, hidden, cols), down_at),
            ],
            out_specs=pl.BlockSpec((rows, hidden), lambda i, at: (0, i)),
        ),
        out_shape=jax.ShapeDtypeStruct((rows, 3 * hidden), LOW),
        name="pack",
    )(t.reshape(1), w_gate_up, w_down)


def unpack_kernel(n_w, shard_ref, *refs):
    pieces, (up_ref, down_ref) = refs[:n_w], refs[n_w:]
    halves, hidden = down_ref.shape[1], pieces[0].shape[1] // 3
    units = halves * hidden
    for s in range(n_w):
        t = lax.rem(shard_ref[0] - s + n_w, n_w)
        j, h = lax.div(t, halves), lax.rem(t, halves)
        for part in range(2):
            at = pl.multiple_of(part * units + h * hidden, 128)
            piece = pieces[s][:, part * hidden : (part + 1) * hidden]
            up_ref[j, :, pl.ds(at, hidden)] = piece.astype(F32)
        down_ref[j, h] = pieces[s][:, 2 * hidden :].astype(F32)


def unpack(pieces, shard, experts):
    n_w = len(pieces)
    rows, hidden = pieces[0].shape[0], pieces[0].shape[1] // 3
    halves = n_w // experts
    cols = hidden
    tile = min(128, rows)
    up, down = pl.pallas_call(
        functools.partial(unpack_kernel, n_w),
        grid_spec=pltpu.PrefetchScalarGridSpec(
            num_scalar_prefetch=1,
            grid=(rows // tile,),
            in_specs=[pl.BlockSpec((tile, 3 * hidden), lambda i, at: (i, 0))] * n_w,
            out_specs=[
                pl.BlockSpec((experts, tile, 2 * halves * hidden), lambda i, at: (0, i, 0)),
                pl.BlockSpec((experts, halves, tile, cols), lambda i, at: (0, 0, i, 0)),
            ],
        ),
        out_shape=[
            jax.ShapeDtypeStruct((experts, rows, 2 * halves * hidden), F32),
            jax.ShapeDtypeStruct((experts, halves, hidden, cols), F32),
        ],
        compiler_params=pltpu.CompilerParams(vmem_limit_bytes=32 * 1024 * 1024),
        name="unpack",
    )(shard.reshape(1), *pieces)
    return up, down.reshape(experts, halves * hidden, cols)


def expert_kernel(experts, n_w, at_ref, place_ref, x_ref, dy_all_ref, used_ref, hot_ref, *refs):
    router_ref, back_router_ref, refs = refs[0], refs[1], refs[2:]
    packs, refs = (refs[:n_w], refs[n_w : 2 * n_w]), refs[2 * n_w :]
    mix_ref, back_ref, dy_ref, dlogits_ref = refs[-8:-4]
    dgu_refs, gated_refs = refs[-4:-2], refs[-2:]
    dy_ref[...] = dy_all_ref[...].reshape(dy_ref.shape)
    hidden = packs[0][0].shape[1] // 3
    cols = packs[0][0].shape[0]
    spans = [pl.ds(pl.multiple_of(at_ref[s] * cols, 128), cols) for s in range(n_w)]
    lane = lax.broadcasted_iota(jnp.int32, (1, router_ref.shape[1]), 1)
    logits = jnp.where(lane < experts, mm(x_ref[...], router_ref[...]), -1e30)
    expo = jnp.exp(logits - jnp.max(logits, axis=-1, keepdims=True))
    gate_all = expo / jnp.sum(expo, axis=-1, keepdims=True)
    used = gate_all * used_ref[...].astype(F32)
    dlogits = jnp.zeros_like(gate_all)
    for h in range(2):
        hot = hot_ref[h : h + 1, :]
        gate = jnp.sum(used * hot, axis=-1, keepdims=True)
        g = u = lifted = 0.0
        for s in range(n_w):
            g = g + mm(x_ref[:, spans[s]], packs[h][s][:, :hidden])
            u = u + mm(x_ref[:, spans[s]], packs[h][s][:, hidden : 2 * hidden])
            lifted = lifted + mm_t(dy_ref[:, spans[s]], packs[h][s][:, 2 * hidden :])
        sigma = jax.nn.sigmoid(g)
        silu = g * sigma
        act = (silu * u).astype(LOW).astype(F32)
        dgate = jnp.sum(act * lifted, axis=-1, keepdims=True)
        gated_refs[h][...] = (act * gate).astype(LOW)
        dact = lifted * gate
        dgu_refs[h][:, :hidden] = (dact * u * (sigma * (1.0 + g * (1.0 - sigma)))).astype(LOW)
        dgu_refs[h][:, hidden:] = (dact * silu).astype(LOW)
        dlogits = dlogits + dgate * gate * (hot - gate_all)
    dlogits = dlogits.astype(LOW)
    dlogits_ref[...] = dlogits
    for s in range(n_w):
        back = mm_t(dgu_refs[0][...], packs[0][s][:, : 2 * hidden])
        back = back + mm_t(dgu_refs[1][...], packs[1][s][:, : 2 * hidden])
        back = back + mm(dlogits, back_router_ref[:, spans[s]])
        back_ref[:, spans[s]] = back.astype(LOW)
    for s in range(n_w):
        mix = mm(gated_refs[0][...], packs[0][s][:, 2 * hidden :])
        mix = mix + mm(gated_refs[1][...], packs[1][s][:, 2 * hidden :])
        mix_ref[:, spans[s]] = mix.astype(LOW)


def expert_pass(x, dy, rows, used, hots, router, packs, at, place, mix, experts):
    n, width = x.shape
    n_w = len(packs[0])
    tile = 2 * rows
    cols, hidden = packs[0][0].shape[0], packs[0][0].shape[1] // 3
    lanes = used.shape[1]

    def tiled(cols):
        return pl.BlockSpec((tile, cols), lambda i, at, place: (i, 0))

    def placed(cols):
        return pl.BlockSpec((tile, cols), lambda i, at, place: (place[i], 0))

    def fixed(shape):
        return pl.BlockSpec(shape, lambda i, at, place: (0, 0), pipeline_mode=pl.Buffered(1))

    outs = [width, width, width, lanes, 2 * hidden, 2 * hidden, hidden, hidden]
    shapes = [jax.ShapeDtypeStruct((n, c), LOW) for c in outs]
    shapes[0] = jax.ShapeDtypeStruct((used.shape[0], width), LOW)
    ins = [x, dy, used, hots, *router, *packs[0], *packs[1]]
    held = [mix] if mix.shape[0] else []
    return pl.pallas_call(
        functools.partial(expert_kernel, experts, n_w),
        grid_spec=pltpu.PrefetchScalarGridSpec(
            num_scalar_prefetch=2,
            grid=(n // tile,),
            in_specs=[
                tiled(width),
                pl.BlockSpec((2, rows, width), lambda i, at, place: (place[i], 0, 0)),
                placed(lanes),
            ]
            + [fixed((2, lanes)), fixed((width, lanes)), fixed((lanes, width))]
            + [fixed((cols, 3 * hidden))] * (2 * n_w)
            + [pl.BlockSpec(memory_space=pl.ANY)] * len(held),
            out_specs=[placed(width)] + [tiled(c) for c in outs[1:]],
        ),
        out_shape=shapes,
        input_output_aliases={len(ins) + 2: 0} if held else {},
        compiler_params=pltpu.CompilerParams(vmem_limit_bytes=56 * 1024 * 1024),
        cost_estimate=LIGHT,
        name="expert_pass",
    )(at, place, *ins, *held)


def grad_kernel(count, shard_ref, *refs):
    hidden = refs[3].shape[1]
    with_router = len(refs) > 4 * count + 1
    each = 5 if with_router else 4
    out_ref = refs[each * count]
    up = down = router = 0.0
    for k in range(count):
        x_ref, dy_ref, dgu_ref, gated_ref = refs[each * k : each * k + 4]
        up = up + t_mm(x_ref[...], dgu_ref[...])
        down = down + t_mm(gated_ref[...], dy_ref[...])
        if with_router:
            router = router + t_mm(x_ref[...], refs[each * k + 4][...])
    out_ref[0, :, : 2 * hidden] = up.astype(out_ref.dtype)
    out_ref[0, :, 2 * hidden :] = down.astype(out_ref.dtype)
    if with_router:
        refs[-1][...] = router


def grad_pass(parts, shard, n_w, kind):
    width = parts[0][0].shape[1]
    hidden = parts[0][3].shape[1]
    cols = width // n_w
    tokens = sum(part[0].shape[0] for part in parts)
    specs = []
    for part in parts:
        n = part[0].shape[0]
        column = pl.BlockSpec((n, cols), lambda i, at: (0, lax.rem(at[0] + i, n_w)))
        specs += [column, column]
        for a in part[2:]:
            specs.append(
                pl.BlockSpec(a.shape, lambda i, at: (0, 0), pipeline_mode=pl.Buffered(1))
            )
    out_specs = [pl.BlockSpec((1, cols, 3 * hidden), lambda i, at: (i, 0, 0))]
    outs = [jax.ShapeDtypeStruct((n_w, cols, 3 * hidden), kind)]
    if len(parts[0]) > 4:
        lanes = parts[0][4].shape[1]
        out_specs.append(pl.BlockSpec((cols, lanes), lambda i, at: (lax.rem(at[0] + i, n_w), 0)))
        outs.append(jax.ShapeDtypeStruct((width, lanes), F32))
    return tuple(
        pl.pallas_call(
            functools.partial(grad_kernel, len(parts)),
            grid_spec=pltpu.PrefetchScalarGridSpec(
                num_scalar_prefetch=1, grid=(n_w,), in_specs=specs, out_specs=out_specs
            ),
            out_shape=outs,
            compiler_params=pltpu.CompilerParams(vmem_limit_bytes=56 * 1024 * 1024),
            cost_estimate=pl.CostEstimate(
                flops=6 * tokens * width * hidden,
                bytes_accessed=4 * tokens * width + 20 * width * hidden,
                transcendentals=0,
            ),
            name="grad_pass",
        )(shard.reshape(1), *[a for part in parts for a in part])
    )


def build(n_e, n_w):
    bits = [1 << b for b in range(n_e.bit_length() - 1)]
    plane = bits[1:]
    nd = len(plane)

    def swap(x, d):
        return lax.ppermute(x, "expert", [(i, i ^ d) for i in range(n_e)])

    def shift(x, s):
        return lax.ppermute(x, "wshard", [(j, (j + s) % n_w) for j in range(n_w)])

    def line_gather(x):
        return [x] + [shift(x, n_w - r) for r in range(1, n_w)]

    def line_scatter(blocks):
        total = blocks[0].astype(F32)
        for r in range(1, n_w):
            total = total + shift(blocks[r], r).astype(F32)
        return total

    def joined(x, d, me):
        got, upper = swap(x, d), (me // d) % 2 == 1
        return jnp.stack([jnp.where(upper, got, x), jnp.where(upper, x, got)])

    def across(x, r):
        return lax.ppermute(x, "wshard", [(j, j ^ r) for j in range(n_w)])

    def pair_parts(x, shard):
        odd = shard % 2 == 1
        blocks = [x] + [across(x, r) for r in range(1, n_w)]
        parts = []
        for a, b in zip(blocks[::2], blocks[1::2]):
            parts.append(jnp.concatenate([jnp.where(odd, b, a), jnp.where(odd, a, b)], 0))
        return parts

    def pair_scatter(parts, shard):
        odd = shard % 2 == 1
        total = 0.0
        for p, part in enumerate(parts):
            a, b = jnp.split(part, 2, 0)
            for r, block in ((2 * p, jnp.where(odd, b, a)), (2 * p + 1, jnp.where(odd, a, b))):
                total = total + (across(block, r) if r else block).astype(F32)
        return total

    def line_exchange(send, shard, order=None):
        got = {0: send(shard)}
        last = None
        for s in order or range(1, n_w):
            x = send((shard + s) % n_w)
            if order and last is not None:
                x = tie(x, last)
            last = got[s] = shift(x, s)
        out = jnp.zeros((n_w,) + got[0].shape, got[0].dtype)
        for s in range(n_w):
            out = lax.dynamic_update_index_in_dim(out, got[s], (shard - s + n_w) % n_w, 0)
        return out

    def line_sum(x, shard):
        x = jnp.roll(x.reshape(2, n_w, -1), shard, axis=1)
        total = x
        for s in range(1, n_w):
            total = total + shift(x, s)
        return jnp.roll(total, -shard, axis=1)

    def way(p, step):
        return plane[(step + p * nd // 2) % nd]

    def plane_gather(parts, early):
        held = [([0], x) for x in parts]
        groups = [held]
        for step in range(nd):
            got = []
            if step == nd - 1:
                arrays, early = both([x for _, x in held], early)
                held = [(masks, x) for (masks, _), x in zip(held, arrays)]
            for p, (masks, x) in enumerate(held):
                got.append(([m | way(p, step) for m in masks], swap(x, way(p, step))))
            groups.append(got)
            held = [
                (a[0] + b[0], jnp.concatenate([a[1], b[1]], 0)) if step + 1 < nd else None
                for a, b in zip(held, got)
            ]
        return groups, early

    def plane_scatter(groups, held):
        mine = [[group[p] for group in groups] for p in range(2)]
        for step in reversed(range(nd)):
            got = [swap(mine[p][step + 1], way(p, step)) for p in range(2)]
            if step == nd - 1:
                got, held = both(got, held())
            for p in range(2):
                at = 0
                for low in range(step + 1):
                    n = mine[p][low].shape[0]
                    total = mine[p][low].astype(F32) + got[p][at : at + n].astype(F32)
                    mine[p][low] = total.astype(LOW)
                    at += n
            (mine,) = both([m[: step + 1] for m in mine])
        return [m[0] for m in mine], held

    def hyper_scatter(x, me, kind, cut=1):
        def halve(x, left, d):
            at = left.index(d)
            bit = (me // d) % 2
            send = lax.dynamic_index_in_dim(x, 1 - bit, at, keepdims=False).astype(kind)
            keep = lax.dynamic_index_in_dim(x, bit, at, keepdims=False)
            return (keep.astype(F32) + swap(send, d).astype(F32)).astype(kind)

        x = x.reshape((2,) * len(bits) + x.shape[1:])
        x = halve(x, list(reversed(bits)), 1)
        parts = []
        for p, part in enumerate(jnp.split(x, cut, -1)):
            left = list(reversed(plane))
            for d in plane[p:] + plane[:p]:
                part = halve(part, left, d)
                left.remove(d)
            parts.append(part)
        return jnp.concatenate(parts, -1)

    def local(
        hidden_in,
        doc_ids,
        routes,
        attn_gain,
        q_gain,
        k_gain,
        ffn_gain,
        w_qkv,
        w_out,
        w_router,
        w_gate_up,
        w_down,
        cotangent,
    ):
        micro = hidden_in.shape[0]
        rows = hidden_in.shape[2]
        width = hidden_in.shape[3]
        heads = HEADS
        head = width // heads
        my_heads = heads // n_w
        cols = width // n_w
        experts = w_router.shape[1]
        local_experts = w_gate_up.shape[0]
        units = w_down.shape[1]
        own = micro * rows
        seq = n_w * rows
        me = lax.axis_index("expert")
        shard = lax.axis_index("wshard")
        scale = head ** (-0.5)

        piece = width // n_w // n_e
        mine = lax.dynamic_slice_in_dim(w_qkv, me * piece, piece, 0)
        mine = mine.reshape(piece, 3, n_w, cols).transpose(2, 0, 1, 3).reshape(n_w, piece, 3 * cols)
        bank = line_exchange(
            lambda t: lax.dynamic_index_in_dim(mine, t, 0, keepdims=False), shard
        )
        upstream = cotangent.reshape(own, width)
        tokens = hidden_in.reshape(own, width).astype(F32)
        scale_one = rms_scale(tokens)
        normed = (tokens * scale_one * attn_gain).astype(LOW)
        used = jnp.any(
            routes.reshape(own, -1, 1) == jnp.arange(experts, dtype=jnp.int32), axis=1
        ).astype(LOW)
        blocks = line_gather(normed)

        rounds = max(1, n_e * n_w * own // 2 // ROUND_TOKENS)
        step = own // rounds
        hidden = units * local_experts // n_w
        arrived = (shard - jnp.arange(n_w, dtype=jnp.int32) + n_w) % n_w
        same = [[2 * c + k for c in range(n_e // 2)] for k in range(2)]
        router_rows = w_router.size // width
        used_rows = step * experts // width

        def rows_for(at):
            rows = [upstream[at : at + step], used[at : at + step].reshape(-1, width)]
            rows = jnp.concatenate(rows + [w_router.reshape(-1, width)], 0)
            return jnp.pad(rows, ((0, -rows.shape[0] % 16), (0, 0)))

        def to_line(rows):
            return lax.all_gather(rows, "wshard")

        def to_pairs(rows):
            rows = lax.all_gather(rows, "expert", axis_index_groups=same)
            return rows.reshape((-1,) + rows.shape[2:])

        pieces = [
            pack_half((shard + k) % n_w, w_gate_up, w_down, n_w // local_experts)
            for k in range(n_w)
        ]
        out_slice = lax.dynamic_slice_in_dim(w_out, me * piece, piece, 0)
        blocks, bank, dy_rows, pieces, out_slice = both(blocks, bank, rows_for(0), pieces, out_slice)

        full_out = line_gather(out_slice)
        dy_rows = to_line(dy_rows)
        first, second = jnp.split(pieces[2], 2, 0)
        first = shift(first, 2)
        normed_all = jnp.concatenate(blocks, 0)

        half = piece // 2
        helds = []
        for p in range(2):
            held = bank[:, p * half : (p + 1) * half]
            for d in plane[p:] + plane[:p]:
                held = joined(held, d, me)
            helds.append(held)
        helds, full_out = both(helds, full_out)
        w_heads = []
        for p, held in enumerate(helds):
            held = joined(held, 1, me)
            dims = plane[p:] + plane[:p] + [1]
            at = {d: len(dims) - 1 - k for k, d in enumerate(dims)}
            k = len(dims)
            w_heads.append(held.transpose(k, *[at[d] for d in reversed(bits)], k + 1, k + 2))
        w_heads = jnp.stack(w_heads, 1 + len(bits)).reshape(width, 3 * cols)
        full_out = jnp.split(jnp.roll(jnp.stack(full_out), shard, axis=0), 2, -1)
        ways = [plane[p:] + plane[:p] + [1] for p in range(2)]
        for step_at, (d0, d1) in enumerate(zip(*ways)):
            full_out = [joined(full_out[0], d0, me), joined(full_out[1], d1, me)]
            if step_at == 0:
                w_heads, full_out, first = both(w_heads, full_out, first)
        orders = [list(reversed(w)) for w in ways]

        projected = mm(normed_all, w_heads)
        squares = jnp.sum(projected.reshape(-1, 3, cols)[:, :2] ** 2, axis=-1).T
        scales = lax.rsqrt(line_sum(squares, shard) / width + EPS)
        scales = scales.reshape(2, -1).T
        projected = projected.reshape(n_w, micro, rows, 3 * cols)
        gains = [lax.dynamic_slice_in_dim(g, shard * cols, cols) for g in (q_gain, k_gain)]
        gains = jnp.stack(gains)
        block_at = (shard + jnp.arange(n_w, dtype=jnp.int32)) % n_w
        positions = block_at[:, None] * rows + jnp.arange(rows, dtype=jnp.int32)[None, :]
        positions = positions.reshape(seq)
        freq = THETA ** (-(jnp.arange(head // 2, dtype=F32) * 2.0 / head))
        angle = positions.astype(F32)[:, None] * freq
        cosine, sine = jnp.cos(angle), jnp.sin(angle)
        cosine = jnp.concatenate([cosine, cosine], 1)
        sine = jnp.concatenate([-sine, sine], 1)
        docs = jnp.take(doc_ids[:, 0], positions, axis=1)
        mask = (positions[None, :] <= positions[:, None])[None] & (
            docs[:, :, None] == docs[:, None, :]
        )
        mask = mask.astype(F32)
        attention = functools.partial(
            attention_call,
            projected,
            scales.reshape(n_w, micro, rows, 2),
            gains,
            cosine,
            sine,
            mask,
        )
        attended = attention().reshape(n_w, own, cols)
        attended, dy_rows, full_out = both(attended, dy_rows, full_out)
        dy_all = to_pairs(dy_rows)
        attended = [shift(attended[r], r) if r else attended[r] for r in range(n_w)]
        resid, ffn_in = out_call(
            out_kernel,
            "out",
            arrived,
            [hidden_in.reshape(own, width), ffn_gain[None]] + attended,
            full_out,
            orders,
            [jax.ShapeDtypeStruct((own, width), F32), jax.ShapeDtypeStruct((own, width), LOW)],
        )

        lanes = -(-experts // 128) * 128
        expert_at = jnp.arange(lanes, dtype=jnp.int32)
        my_expert = local_experts * me + shard * local_experts // n_w
        sib_expert = local_experts * jnp.bitwise_xor(me, 1) + shard * local_experts // n_w
        hots = jnp.stack([(expert_at == e).astype(F32) for e in (my_expert, sib_expert)])

        def whole(groups):
            return jnp.concatenate([b for group in groups for _, b in group], 0)

        dffn, mixture = [], []
        grads = None
        for n in range(rounds):
            at = n * step
            ffn_rows = ffn_in[at : at + step]
            if n:
                ffn_rows, grads, dffn, mixture = lax.optimization_barrier(
                    (ffn_rows, grads, dffn, mixture)
                )
                dy_all = to_pairs(to_line(tie(rows_for(at), ffn_rows)))
            parts = pair_parts(ffn_rows, shard)
            if n == 0:
                parts, pieces, second = both(parts, pieces, second)
                pieces[1] = shift(pieces[1], 1)
            mask = dy_all[:, step : step + used_rows].reshape(-1, experts)
            mask = jnp.pad(mask, ((0, 0), (0, lanes - experts)))
            router = dy_all[:n_w, step + used_rows : step + used_rows + router_rows]
            router = jnp.pad(router.reshape(width, experts), ((0, 0), (0, lanes - experts)))
            groups, (mask, router, router_t, pieces) = plane_gather(
                parts, (mask, router, router.T, pieces)
            )
            waves = [groups]
            xs = [whole(wave) for wave in waves]
            places = [
                jnp.stack(
                    [
                        jnp.bitwise_xor(me // 2, m // 2) * (n_w // 2)
                        + jnp.bitwise_xor(shard // 2, p)
                        for group in wave
                        for p in range(2)
                        for m in group[p][0]
                    ]
                )
                for wave in waves
            ]
            if n == 0:
                pieces[3] = shift(pieces[3], 3)
                pieces[2] = jnp.concatenate([first, shift(second, 2)], 0)
                packs = [pieces, [swap(piece, 1) for piece in pieces]]
            mix = jnp.zeros((0, width), LOW)
            back, passed = [], []
            for wave, x, place in zip(waves, xs, places):
                mix, part, *rest = expert_pass(
                    x, dy_all, step, mask, hots, (router, router_t), packs, arrived, place, mix, experts
                )
                cuts = []
                for group in wave:
                    for p in range(2):
                        cuts.append((cuts[-1] if cuts else 0) + group[p][1].shape[0])
                part = jnp.split(part, cuts[:-1], 0)
                back += [part[2 * g : 2 * g + 2] for g in range(len(wave))]
                passed.append([x] + rest)
            kind = LOW if rounds == 1 else F32
            def weight_grads():
                ins = [[x, dy, dgu1, gated1, dlogits] for x, dy, dlogits, _, dgu1, _, gated1 in passed]
                sib = grad_pass(ins, shard, n_w, kind)
                ins = [[x, dy, dgu0, gated0] for x, dy, _, dgu0, _, gated0, _ in passed]
                return sib + grad_pass(ins, shard, n_w, kind)

            back, new = plane_scatter(back, weight_grads)
            grads = new if grads is None else jax.tree.map(jnp.add, grads, new)
            grad_sib, grad_router, grad_own = grads
            if n == rounds - 1:
                grad_sib = swap(grad_sib.astype(LOW), 1)
                sums = [
                    (grad_own[s].astype(F32) + grad_sib[s].astype(F32)).astype(LOW)
                    for s in range(n_w)
                ]
                sums[1] = shift(sums[1], 1)
                back, sums[1] = both(back, sums[1])
            back, mix = both(back, mix)
            dffn.append(pair_scatter(back, shard))
            mixture.append(
                lax.psum_scatter(mix, "expert", axis_index_groups=same, tiled=True)
            )
        dffn = jnp.concatenate(dffn, 0)
        grad_router = grad_router[:, :experts]

        piece_type = jax.ShapeDtypeStruct((own, cols), LOW)
        dresid, dbranch, grad_ffn_gain, *dattended = out_call(
            out_back_kernel,
            "out_back",
            arrived,
            [dffn, resid, upstream, ffn_gain[None]],
            full_out,
            orders,
            [
                jax.ShapeDtypeStruct((own, width), F32),
                jax.ShapeDtypeStruct((own, width), LOW),
                jax.ShapeDtypeStruct((1, width), F32),
            ]
            + [piece_type] * n_w,
        )
        dattended = [shift(x, n_w - r) if r else x for r, x in enumerate(dattended)]
        dattended = jnp.concatenate(dattended, 0)
        third, fourth = jnp.split(sums[3], 2, 0)
        third = shift(third, 3)
        dq, dk, dv, inners, grad_gains = attention(dattended.reshape(n_w, micro, rows, cols))
        dbranch, inners, mixture, third = both(dbranch, inners, mixture, third)
        mixture = [lax.psum_scatter(m, "wshard", tiled=True).astype(F32) for m in mixture]
        (grad_out,) = out_call(
            out_grad_kernel,
            "out_grad",
            arrived,
            [dbranch] + attended,
            [],
            orders,
            [jax.ShapeDtypeStruct((width, width), LOW)],
        )
        inners = line_sum(jnp.sum(inners, 0).reshape(-1, 2).T, shard) / width
        inners, fourth = both(inners, fourth)
        fourth = shift(fourth, 3)
        inners = inners.reshape(2, -1).T
        flat = projected.reshape(-1, 3 * cols)
        dproj = jnp.concatenate(
            [
                norm_back(
                    flat[:, p * cols : (p + 1) * cols],
                    scales[:, p : p + 1],
                    gains[p],
                    d.reshape(-1, cols),
                    inners[:, p : p + 1],
                ).astype(LOW)
                for p, d in enumerate((dq, dk))
            ]
            + [dv.reshape(-1, cols)],
            1,
        )
        dnormed = mm_t(dproj, w_heads).astype(LOW)
        dnormed, fourth = both(dnormed, fourth)
        sums[3] = jnp.concatenate([third, fourth], 0)
        dnormed = dnormed.reshape(n_w, own, width)
        dnormed = line_scatter([dnormed[r] for r in range(n_w)])
        dnormed, sums[2], grad_out, dproj = both(dnormed, sums[2], grad_out, dproj)
        sums[2] = shift(sums[2], 2)
        small = width // (n_e * n_w)
        out_part = hyper_scatter(grad_out.reshape(n_e, n_w * small, width), me, LOW, nd)
        out_part = out_part.reshape(n_w, small, width)
        out_rows = 0.0
        for k in range(n_w):
            block = lax.dynamic_index_in_dim(out_part, (shard + k) % n_w, 0, keepdims=False)
            out_rows = out_rows + (shift(block, k) if k else block).astype(F32)
        inner = jnp.mean(tokens * (attn_gain * dnormed), axis=-1, keepdims=True)
        dx = norm_back(tokens, scale_one, attn_gain, dnormed, inner)
        grad_in = (dresid + dx).astype(LOW)
        mixture = jnp.concatenate(mixture, 0)
        hidden_out = (resid + mixture).astype(LOW)
        grad_qkv = t_mm(normed_all, dproj)
        grad_attn_gain = jnp.sum(grad_qkv * w_heads.astype(F32), axis=1) / attn_gain

        qkv = hyper_scatter(grad_qkv.reshape(n_e, n_w * small, 3 * cols), me, LOW, nd)
        qkv, sums[2] = both(qkv.reshape(n_w, small, 3 * cols), sums[2])
        arrivals = []
        for k in range(n_w):
            rows_k = lax.dynamic_index_in_dim(qkv, (shard + k) % n_w, 0, keepdims=False)
            arrivals.append(shift(rows_k, k) if k else rows_k)
        out_qkv = spread(arrivals, shard)
        out_gate_up, out_down = unpack(sums, shard, local_experts)
        def all_scatter(x):
            x = x.reshape(-1, n_e, n_w * small).transpose(1, 0, 2)
            x = hyper_scatter(x, me, F32).reshape(-1, n_w, small)
            total = lax.dynamic_index_in_dim(x, shard, 1, keepdims=False)
            for s in range(1, n_w):
                send = lax.dynamic_index_in_dim(x, (shard + s) % n_w, 1, keepdims=False)
                total = total + shift(send, s)
            return total

        gains = jnp.zeros((2, width), F32)
        gains = lax.dynamic_update_slice(gains, jnp.sum(grad_gains, 0), (0, shard * cols))
        pack = [gains, grad_attn_gain[None], grad_ffn_gain, grad_router.T]
        pack, dnormed = both(jnp.concatenate(pack, 0), dnormed)
        pack = all_scatter(pack)
        return (
            hidden_out.reshape(micro, 1, rows, width),
            grad_in.reshape(micro, 1, rows, width),
            pack[2],
            pack[0],
            pack[1],
            pack[3],
            out_qkv,
            out_rows,
            pack[4:].T,
            out_gate_up,
            out_down,
        )

    return local


def solution(mesh):
    in_specs = (
        P(None, "expert", "wshard", None),
        P(None, "expert", None),
        P(None, "expert", "wshard", None),
        P(),
        P(),
        P(),
        P(),
        P("wshard", None),
        P("wshard", None),
        P("wshard", None),
        P("expert", "wshard", None),
        P("expert", None, "wshard"),
        P(None, "expert", "wshard", None),
    )
    out_specs = (
        P(None, "expert", "wshard", None),
        P(None, "expert", "wshard", None),
        P(("expert", "wshard")),
        P(("expert", "wshard")),
        P(("expert", "wshard")),
        P(("expert", "wshard")),
        P(("expert", "wshard"), None),
        P(("expert", "wshard"), None),
        P(("expert", "wshard"), None),
        P("expert", "wshard", None),
        P("expert", None, "wshard"),
    )
    local = build(mesh.shape["expert"], mesh.shape["wshard"])
    return jax.shard_map(local, mesh=mesh, in_specs=in_specs, out_specs=out_specs, check_vma=False)
```

```python
import functools

import jax
import jax.numpy as jnp
from jax import lax
from jax.experimental import pallas as pl
from jax.experimental.pallas import tpu as pltpu
from jax.sharding import PartitionSpec as P

HEADS = 16
EPS = 1e-05
THETA = 10000.0
ROUND_TOKENS = 2048
AXES = ("expert", "wshard")
LOW = jnp.bfloat16
F32 = jnp.float32


def rms_scale(values):
    return lax.rsqrt(jnp.mean(values * values, axis=-1, keepdims=True) + EPS)


def norm_back(values, scale, gain, grads, inner):
    weighted = gain * grads
    return scale * weighted - values * scale * scale * scale * inner


def dot(a, b, dims):
    return lax.dot_general(a, b, (dims, ((), ())), preferred_element_type=F32)


def mm(a, b):
    return dot(a, b, ((1,), (0,)))


def mm_t(a, b):
    return dot(a, b, ((1,), (1,)))


def t_mm(a, b):
    return dot(a, b, ((0,), (0,)))


def both(*arrays):
    return lax.optimization_barrier(arrays)


def tie(x, *after):
    return lax.optimization_barrier((x, after))[0]


def spread_kernel(n_w, shard_ref, *refs):
    out_ref = refs[-1]
    cols = refs[0].shape[1] // 3
    for s in range(n_w):
        t = lax.rem(shard_ref[0] - s + n_w, n_w)
        for part in range(3):
            at = pl.multiple_of((part * n_w + t) * cols, 128)
            out_ref[:, pl.ds(at, cols)] = refs[s][:, part * cols : (part + 1) * cols].astype(F32)


def spread(pieces, shard):
    n_w = len(pieces)
    rows, width = pieces[0].shape
    return pl.pallas_call(
        functools.partial(spread_kernel, n_w),
        grid_spec=pltpu.PrefetchScalarGridSpec(
            num_scalar_prefetch=1,
            grid=(1,),
            in_specs=[pl.BlockSpec((rows, width), lambda i, at: (0, 0))] * n_w,
            out_specs=pl.BlockSpec((rows, n_w * width), lambda i, at: (0, 0)),
        ),
        out_shape=jax.ShapeDtypeStruct((rows, n_w * width), F32),
        name="spread",
    )(shard.reshape(1), *pieces)


LIGHT = pl.CostEstimate(flops=1, bytes_accessed=1, transcendentals=0)


def turned(x, cos_ref, sin_ref, sign):
    return x * cos_ref[...] + sign * pltpu.roll(x, x.shape[1] // 2, 1) * sin_ref[...]


def attention_parts(q_ref, k_ref, v_ref, scale_ref, gain_ref, cos_ref, sin_ref, mask_ref):
    seq, head = cos_ref.shape
    raw_q = q_ref[:, 0].reshape(seq, head)
    raw_k = k_ref[:, 0].reshape(seq, head)
    values = v_ref[:, 0].reshape(seq, head).astype(LOW)
    scales = scale_ref[:, 0].reshape(seq, 2)
    hat_q = raw_q * scales[:, 0:1] * gain_ref[0:1, :]
    hat_k = raw_k * scales[:, 1:2] * gain_ref[1:2, :]
    queries = turned(hat_q, cos_ref, sin_ref, 1.0).astype(LOW)
    keys = turned(hat_k, cos_ref, sin_ref, 1.0).astype(LOW)
    scores = mm_t(queries, keys) * head ** (-0.5)
    scores = jnp.where(mask_ref[0] > 0, scores, -1e30)
    expo = jnp.exp(scores - jnp.max(scores, axis=-1, keepdims=True))
    probs = expo / jnp.sum(expo, axis=-1, keepdims=True)
    return raw_q, raw_k, values, scales, queries, keys, probs


def attention_kernel(*refs):
    out_ref = refs[-1]
    _, _, values, _, _, _, probs = attention_parts(*refs[:-1])
    out = mm(probs.astype(LOW), values).astype(LOW)
    out_ref[...] = out.reshape(out_ref.shape)


def attention_back_kernel(*refs):
    grad_ref, (dq_ref, dk_ref, dv_ref, inner_ref, gains_ref) = refs[8], refs[9:]
    gain_ref, cos_ref, sin_ref = refs[4:7]
    raw_q, raw_k, values, scales, queries, keys, probs = attention_parts(*refs[:8])
    seq, head = cos_ref.shape
    grad = grad_ref[:, 0].reshape(seq, head)
    dprobs = mm_t(grad, values)
    dscores = probs * (dprobs - jnp.sum(probs * dprobs, axis=-1, keepdims=True))
    dscores = dscores.astype(LOW)
    dq = turned(mm(dscores, keys) * head ** (-0.5), cos_ref, sin_ref, -1.0)
    dk = turned(t_mm(dscores, queries) * head ** (-0.5), cos_ref, sin_ref, -1.0)
    dv = t_mm(probs.astype(LOW), grad)
    dq_ref[...] = dq.reshape(dq_ref.shape)
    dk_ref[...] = dk.reshape(dk_ref.shape)
    dv_ref[...] = dv.astype(LOW).reshape(dv_ref.shape)
    inner_q = jnp.sum(raw_q * gain_ref[0:1, :] * dq, axis=-1, keepdims=True)
    inner_k = jnp.sum(raw_k * gain_ref[1:2, :] * dk, axis=-1, keepdims=True)
    inner_ref[...] = jnp.concatenate([inner_q, inner_k], 1).reshape(inner_ref.shape)
    gains_ref[0, 0:1, :] = jnp.sum(dq * raw_q * scales[:, 0:1], axis=0, keepdims=True)
    gains_ref[0, 1:2, :] = jnp.sum(dk * raw_k * scales[:, 1:2], axis=0, keepdims=True)


def attention_call(projected, scales, gains, cosine, sine, mask, grad=None):
    n_w, micro, rows, cols = projected.shape
    seq, head = cosine.shape
    cols = cols // 3
    heads = cols // head

    def part(p):
        return pl.BlockSpec((n_w, 1, rows, head), lambda m, h: (0, m, 0, p * heads + h))

    fixed = pl.BlockSpec((seq, head), lambda m, h: (0, 0))
    specs = [part(0), part(1), part(2)]
    specs.append(pl.BlockSpec((n_w, 1, rows, 2), lambda m, h: (0, m, 0, 0)))
    specs.append(pl.BlockSpec((2, head), lambda m, h: (0, h)))
    specs += [fixed, fixed, pl.BlockSpec((1, seq, seq), lambda m, h: (m, 0, 0))]
    ins = [projected] * 3 + [scales, gains, cosine, sine, mask]

    def like(kind):
        return jax.ShapeDtypeStruct((n_w, micro, rows, cols), kind)

    if grad is None:
        kernel, outs, out_specs = attention_kernel, like(LOW), part(0)
    else:
        ins, specs = ins + [grad], specs + [part(0)]
        kernel = attention_back_kernel
        outs = [
            like(F32),
            like(F32),
            like(LOW),
            jax.ShapeDtypeStruct((heads, n_w, micro, rows, 2), F32),
            jax.ShapeDtypeStruct((micro, 2, cols), F32),
        ]
        out_specs = [part(0)] * 3 + [
            pl.BlockSpec((1, n_w, 1, rows, 2), lambda m, h: (h, 0, m, 0, 0)),
            pl.BlockSpec((1, 2, head), lambda m, h: (m, 0, h)),
        ]
    return pl.pallas_call(
        kernel,
        grid=(micro, heads),
        in_specs=specs,
        out_specs=out_specs,
        out_shape=outs,
        compiler_params=pltpu.CompilerParams(vmem_limit_bytes=32 * 1024 * 1024),
        cost_estimate=LIGHT,
        name="attention" if grad is None else "attention_back",
    )(*ins)


def plane_rows(ref, order):
    picks = range(1 << len(order))
    return jnp.concatenate([ref[tuple((i // d) % 2 for d in order) + (0,)] for i in picks], 0)


def out_kernel(n_w, orders, at_ref, x_ref, gain_ref, *refs):
    pieces, weights, (resid_ref, ffn_ref) = refs[:n_w], refs[n_w : 3 * n_w], refs[3 * n_w :]
    total = []
    for p, order in enumerate(orders):
        half = weights[0].shape[-1]
        part = x_ref[:, p * half : (p + 1) * half].astype(F32)
        for s in range(n_w):
            part = part + mm(pieces[s][...], plane_rows(weights[p * n_w + s], order))
        total.append(part)
    total = jnp.concatenate(total, 1)
    resid_ref[...] = total
    ffn_ref[...] = (total * rms_scale(total) * gain_ref[...]).astype(LOW)


def out_back_kernel(n_w, orders, at_ref, dffn_ref, resid_ref, dy_ref, gain_ref, *refs):
    weights, (dresid_ref, low_ref, sum_ref) = refs[: 2 * n_w], refs[2 * n_w : 2 * n_w + 3]
    outs = refs[2 * n_w + 3 :]
    dffn, resid = dffn_ref[...], resid_ref[...]
    scale = rms_scale(resid)
    weighted = gain_ref[...] * dffn
    inner = jnp.mean(resid * weighted, axis=-1, keepdims=True)
    dresid = dy_ref[...].astype(F32) + norm_back(resid, scale, gain_ref[...], dffn, inner)
    dresid_ref[...] = dresid
    low_ref[...] = dresid.astype(LOW)
    sum_ref[...] = jnp.sum(dffn * resid * scale, axis=0, keepdims=True)
    for s in range(n_w):
        total = 0.0
        for p, order in enumerate(orders):
            half = weights[0].shape[-1]
            weight = plane_rows(weights[p * n_w + s], order)
            total = total + mm_t(low_ref[:, p * half : (p + 1) * half], weight)
        outs[s][...] = total.astype(LOW)


def out_grad_kernel(n_w, orders, at_ref, low_ref, *refs):
    pieces, out_ref = refs[:n_w], refs[n_w]
    cols = pieces[0].shape[1]
    for s in range(n_w):
        rows = pl.ds(pl.multiple_of(at_ref[s] * cols, 128), cols)
        out_ref[rows, :] = t_mm(pieces[s][...], low_ref[...]).astype(LOW)


def out_call(kernel, name, at, ins, weights, orders, outs):
    n_w = at.shape[0]

    def fixed(shape):
        return pl.BlockSpec(shape, lambda i, at: (0,) * len(shape))

    specs = [fixed(a.shape) for a in ins]
    for weight in weights:
        lead = weight.ndim - 3
        shape = weight.shape[:lead] + (1,) + weight.shape[-2:]
        for s in range(n_w):
            specs.append(
                pl.BlockSpec(shape, lambda i, at, s=s, lead=lead: (0,) * lead + (at[s], 0, 0))
            )
        ins = ins + [weight] * n_w
    return pl.pallas_call(
        functools.partial(kernel, n_w, orders),
        grid_spec=pltpu.PrefetchScalarGridSpec(
            num_scalar_prefetch=1,
            grid=(1,),
            in_specs=specs,
            out_specs=[fixed(o.shape) for o in outs],
        ),
        out_shape=outs,
        compiler_params=pltpu.CompilerParams(vmem_limit_bytes=56 * 1024 * 1024),
        cost_estimate=LIGHT,
        name=name,
    )(at, *ins)


def pack_kernel(at_ref, up_ref, down_ref, out_ref):
    step = pl.program_id(0)

    @pl.when(step < 2)
    def _():
        out_ref[...] = up_ref[0]

    @pl.when(step == 2)
    def _():
        out_ref[...] = down_ref[0]


def pack_half(t, w_gate_up, w_down, halves):
    rows = w_gate_up.shape[1]
    hidden = w_down.shape[1] // halves
    cols = w_down.shape[2]

    def up_at(i, at):
        return (at[0] // halves, 0, jnp.minimum(i, 1) * halves + at[0] % halves)

    def down_at(i, at):
        return (at[0] // halves, at[0] % halves, 0)

    return pl.pallas_call(
        pack_kernel,
        grid_spec=pltpu.PrefetchScalarGridSpec(
            num_scalar_prefetch=1,
            grid=(3,),
            in_specs=[
                pl.BlockSpec((1, rows, hidden), up_at),
                pl.BlockSpec((1, hidden, cols), down_at),
            ],
            out_specs=pl.BlockSpec((rows, hidden), lambda i, at: (0, i)),
        ),
        out_shape=jax.ShapeDtypeStruct((rows, 3 * hidden), LOW),
        name="pack",
    )(t.reshape(1), w_gate_up, w_down)


def unpack_kernel(n_w, shard_ref, *refs):
    pieces, (up_ref, down_ref) = refs[:n_w], refs[n_w:]
    halves, hidden = down_ref.shape[1], pieces[0].shape[1] // 3
    units = halves * hidden
    for s in range(n_w):
        t = lax.rem(shard_ref[0] - s + n_w, n_w)
        j, h = lax.div(t, halves), lax.rem(t, halves)
        for part in range(2):
            at = pl.multiple_of(part * units + h * hidden, 128)
            piece = pieces[s][:, part * hidden : (part + 1) * hidden]
            up_ref[j, :, pl.ds(at, hidden)] = piece.astype(F32)
        down_ref[j, h] = pieces[s][:, 2 * hidden :].astype(F32)


def unpack(pieces, shard, experts):
    n_w = len(pieces)
    rows, hidden = pieces[0].shape[0], pieces[0].shape[1] // 3
    halves = n_w // experts
    cols = hidden
    tile = min(128, rows)
    up, down = pl.pallas_call(
        functools.partial(unpack_kernel, n_w),
        grid_spec=pltpu.PrefetchScalarGridSpec(
            num_scalar_prefetch=1,
            grid=(rows // tile,),
            in_specs=[pl.BlockSpec((tile, 3 * hidden), lambda i, at: (i, 0))] * n_w,
            out_specs=[
                pl.BlockSpec((experts, tile, 2 * halves * hidden), lambda i, at: (0, i, 0)),
                pl.BlockSpec((experts, halves, tile, cols), lambda i, at: (0, 0, i, 0)),
            ],
        ),
        out_shape=[
            jax.ShapeDtypeStruct((experts, rows, 2 * halves * hidden), F32),
            jax.ShapeDtypeStruct((experts, halves, hidden, cols), F32),
        ],
        compiler_params=pltpu.CompilerParams(vmem_limit_bytes=32 * 1024 * 1024),
        name="unpack",
    )(shard.reshape(1), *pieces)
    return up, down.reshape(experts, halves * hidden, cols)


def expert_kernel(experts, n_w, at_ref, place_ref, x_ref, dy_all_ref, used_ref, hot_ref, *refs):
    router_ref, back_router_ref, refs = refs[0], refs[1], refs[2:]
    packs, refs = (refs[:n_w], refs[n_w : 2 * n_w]), refs[2 * n_w :]
    mix_ref, back_ref, dy_ref, dlogits_ref = refs[-8:-4]
    dgu_refs, gated_refs = refs[-4:-2], refs[-2:]
    dy_ref[...] = dy_all_ref[...].reshape(dy_ref.shape)
    hidden = packs[0][0].shape[1] // 3
    cols = packs[0][0].shape[0]
    spans = [pl.ds(pl.multiple_of(at_ref[s] * cols, 128), cols) for s in range(n_w)]
    lane = lax.broadcasted_iota(jnp.int32, (1, router_ref.shape[1]), 1)
    logits = jnp.where(lane < experts, mm(x_ref[...], router_ref[...]), -1e30)
    expo = jnp.exp(logits - jnp.max(logits, axis=-1, keepdims=True))
    gate_all = expo / jnp.sum(expo, axis=-1, keepdims=True)
    used = gate_all * used_ref[...].astype(F32)
    dlogits = jnp.zeros_like(gate_all)
    for h in range(2):
        hot = hot_ref[h : h + 1, :]
        gate = jnp.sum(used * hot, axis=-1, keepdims=True)
        g = u = lifted = 0.0
        for s in range(n_w):
            g = g + mm(x_ref[:, spans[s]], packs[h][s][:, :hidden])
            u = u + mm(x_ref[:, spans[s]], packs[h][s][:, hidden : 2 * hidden])
            lifted = lifted + mm_t(dy_ref[:, spans[s]], packs[h][s][:, 2 * hidden :])
        sigma = jax.nn.sigmoid(g)
        silu = g * sigma
        act = (silu * u).astype(LOW).astype(F32)
        dgate = jnp.sum(act * lifted, axis=-1, keepdims=True)
        gated_refs[h][...] = (act * gate).astype(LOW)
        dact = lifted * gate
        dgu_refs[h][:, :hidden] = (dact * u * (sigma * (1.0 + g * (1.0 - sigma)))).astype(LOW)
        dgu_refs[h][:, hidden:] = (dact * silu).astype(LOW)
        dlogits = dlogits + dgate * gate * (hot - gate_all)
    dlogits = dlogits.astype(LOW)
    dlogits_ref[...] = dlogits
    for s in range(n_w):
        back = mm_t(dgu_refs[0][...], packs[0][s][:, : 2 * hidden])
        back = back + mm_t(dgu_refs[1][...], packs[1][s][:, : 2 * hidden])
        back = back + mm(dlogits, back_router_ref[:, spans[s]])
        back_ref[:, spans[s]] = back.astype(LOW)
    for s in range(n_w):
        mix = mm(gated_refs[0][...], packs[0][s][:, 2 * hidden :])
        mix = mix + mm(gated_refs[1][...], packs[1][s][:, 2 * hidden :])
        mix_ref[:, spans[s]] = mix.astype(LOW)


def expert_pass(x, dy, rows, used, hots, router, packs, at, place, mix, experts):
    n, width = x.shape
    n_w = len(packs[0])
    tile = 2 * rows
    cols, hidden = packs[0][0].shape[0], packs[0][0].shape[1] // 3
    lanes = used.shape[1]

    def tiled(cols):
        return pl.BlockSpec((tile, cols), lambda i, at, place: (i, 0))

    def placed(cols):
        return pl.BlockSpec((tile, cols), lambda i, at, place: (place[i], 0))

    def fixed(shape):
        return pl.BlockSpec(shape, lambda i, at, place: (0, 0), pipeline_mode=pl.Buffered(1))

    outs = [width, width, width, lanes, 2 * hidden, 2 * hidden, hidden, hidden]
    shapes = [jax.ShapeDtypeStruct((n, c), LOW) for c in outs]
    shapes[0] = jax.ShapeDtypeStruct((used.shape[0], width), LOW)
    ins = [x, dy, used, hots, *router, *packs[0], *packs[1]]
    held = [mix] if mix.shape[0] else []
    return pl.pallas_call(
        functools.partial(expert_kernel, experts, n_w),
        grid_spec=pltpu.PrefetchScalarGridSpec(
            num_scalar_prefetch=2,
            grid=(n // tile,),
            in_specs=[
                tiled(width),
                pl.BlockSpec((2, rows, width), lambda i, at, place: (place[i], 0, 0)),
                placed(lanes),
            ]
            + [fixed((2, lanes)), fixed((width, lanes)), fixed((lanes, width))]
            + [fixed((cols, 3 * hidden))] * (2 * n_w)
            + [pl.BlockSpec(memory_space=pl.ANY)] * len(held),
            out_specs=[placed(width)] + [tiled(c) for c in outs[1:]],
        ),
        out_shape=shapes,
        input_output_aliases={len(ins) + 2: 0} if held else {},
        compiler_params=pltpu.CompilerParams(vmem_limit_bytes=56 * 1024 * 1024),
        cost_estimate=LIGHT,
        name="expert_pass",
    )(at, place, *ins, *held)


def grad_kernel(count, shard_ref, *refs):
    hidden = refs[3].shape[1]
    with_router = len(refs) > 4 * count + 1
    each = 5 if with_router else 4
    out_ref = refs[each * count]
    up = down = router = 0.0
    for k in range(count):
        x_ref, dy_ref, dgu_ref, gated_ref = refs[each * k : each * k + 4]
        up = up + t_mm(x_ref[...], dgu_ref[...])
        down = down + t_mm(gated_ref[...], dy_ref[...])
        if with_router:
            router = router + t_mm(x_ref[...], refs[each * k + 4][...])
    out_ref[0, :, : 2 * hidden] = up.astype(out_ref.dtype)
    out_ref[0, :, 2 * hidden :] = down.astype(out_ref.dtype)
    if with_router:
        refs[-1][0] = router


def grad_pass(parts, shard, n_w, kind, first, count):
    width = parts[0][0].shape[1]
    hidden = parts[0][3].shape[1]
    cols = width // n_w
    tokens = sum(part[0].shape[0] for part in parts)
    specs = []
    for part in parts:
        n = part[0].shape[0]
        column = pl.BlockSpec((n, cols), lambda i, at: (0, lax.rem(at[0] + first + i, n_w)))
        specs += [column, column]
        for a in part[2:]:
            specs.append(
                pl.BlockSpec(a.shape, lambda i, at: (0, 0), pipeline_mode=pl.Buffered(1))
            )
    out_specs = [pl.BlockSpec((1, cols, 3 * hidden), lambda i, at: (i, 0, 0))]
    outs = [jax.ShapeDtypeStruct((count, cols, 3 * hidden), kind)]
    if len(parts[0]) > 4:
        lanes = parts[0][4].shape[1]
        out_specs.append(pl.BlockSpec((1, cols, lanes), lambda i, at: (i, 0, 0)))
        outs.append(jax.ShapeDtypeStruct((count, cols, lanes), F32))
    return tuple(
        pl.pallas_call(
            functools.partial(grad_kernel, len(parts)),
            grid_spec=pltpu.PrefetchScalarGridSpec(
                num_scalar_prefetch=1, grid=(count,), in_specs=specs, out_specs=out_specs
            ),
            out_shape=outs,
            compiler_params=pltpu.CompilerParams(vmem_limit_bytes=56 * 1024 * 1024),
            cost_estimate=pl.CostEstimate(
                flops=6 * tokens * cols * count * hidden,
                bytes_accessed=4 * tokens * width + 20 * width * hidden,
                transcendentals=0,
            ),
            name="grad_pass",
        )(shard.reshape(1), *[a for part in parts for a in part])
    )


def build(n_e, n_w):
    bits = [1 << b for b in range(n_e.bit_length() - 1)]
    plane = bits[1:]
    nd = len(plane)

    def swap(x, d):
        return lax.ppermute(x, "expert", [(i, i ^ d) for i in range(n_e)])

    def shift(x, s):
        return lax.ppermute(x, "wshard", [(j, (j + s) % n_w) for j in range(n_w)])

    def line_gather(x):
        return [x] + [shift(x, n_w - r) for r in range(1, n_w)]

    def line_scatter(blocks):
        total = blocks[0].astype(F32)
        for r in range(1, n_w):
            total = total + shift(blocks[r], r).astype(F32)
        return total

    def joined(x, d, me):
        got, upper = swap(x, d), (me // d) % 2 == 1
        return jnp.stack([jnp.where(upper, got, x), jnp.where(upper, x, got)])

    def across(x, r):
        return lax.ppermute(x, "wshard", [(j, j ^ r) for j in range(n_w)])

    def pair_parts(x, shard):
        odd = shard % 2 == 1
        blocks = [x] + [across(x, r) for r in range(1, n_w)]
        parts = []
        for a, b in zip(blocks[::2], blocks[1::2]):
            parts.append(jnp.concatenate([jnp.where(odd, b, a), jnp.where(odd, a, b)], 0))
        return parts

    def pair_scatter(parts, shard):
        odd = shard % 2 == 1
        total = 0.0
        for p, part in enumerate(parts):
            a, b = jnp.split(part, 2, 0)
            for r, block in ((2 * p, jnp.where(odd, b, a)), (2 * p + 1, jnp.where(odd, a, b))):
                total = total + (across(block, r) if r else block).astype(F32)
        return total

    def line_exchange(send, shard, order=None):
        got = {0: send(shard)}
        last = None
        for s in order or range(1, n_w):
            x = send((shard + s) % n_w)
            if order and last is not None:
                x = tie(x, last)
            last = got[s] = shift(x, s)
        out = jnp.zeros((n_w,) + got[0].shape, got[0].dtype)
        for s in range(n_w):
            out = lax.dynamic_update_index_in_dim(out, got[s], (shard - s + n_w) % n_w, 0)
        return out

    def line_sum(x, shard):
        x = jnp.roll(x.reshape(2, n_w, -1), shard, axis=1)
        total = x
        for s in range(1, n_w):
            total = total + shift(x, s)
        return jnp.roll(total, -shard, axis=1)

    def way(p, step):
        return plane[(step + p * nd // 2) % nd]

    def plane_gather(parts, early):
        held = [([0], x) for x in parts]
        groups = [held]
        for step in range(nd):
            got = []
            if step == nd - 1:
                arrays, early = both([x for _, x in held], early)
                held = [(masks, x) for (masks, _), x in zip(held, arrays)]
            for p, (masks, x) in enumerate(held):
                got.append(([m | way(p, step) for m in masks], swap(x, way(p, step))))
            groups.append(got)
            held = [
                (a[0] + b[0], jnp.concatenate([a[1], b[1]], 0)) if step + 1 < nd else None
                for a, b in zip(held, got)
            ]
        return groups, early

    def plane_scatter(groups, held):
        mine = [[group[p] for group in groups] for p in range(2)]
        for step in reversed(range(nd)):
            got = [swap(mine[p][step + 1], way(p, step)) for p in range(2)]
            if step == nd - 1:
                got, held = both(got, held())
            for p in range(2):
                at = 0
                for low in range(step + 1):
                    n = mine[p][low].shape[0]
                    total = mine[p][low].astype(F32) + got[p][at : at + n].astype(F32)
                    mine[p][low] = total.astype(LOW)
                    at += n
            (mine,) = both([m[: step + 1] for m in mine])
        return [m[0] for m in mine], held

    def hyper_scatter(x, me, kind, cut=1):
        def halve(x, left, d):
            at = left.index(d)
            bit = (me // d) % 2
            send = lax.dynamic_index_in_dim(x, 1 - bit, at, keepdims=False).astype(kind)
            keep = lax.dynamic_index_in_dim(x, bit, at, keepdims=False)
            return (keep.astype(F32) + swap(send, d).astype(F32)).astype(kind)

        x = x.reshape((2,) * len(bits) + x.shape[1:])
        x = halve(x, list(reversed(bits)), 1)
        parts = []
        for p, part in enumerate(jnp.split(x, cut, -1)):
            left = list(reversed(plane))
            for d in plane[p:] + plane[:p]:
                part = halve(part, left, d)
                left.remove(d)
            parts.append(part)
        return jnp.concatenate(parts, -1)

    def local(
        hidden_in,
        doc_ids,
        routes,
        attn_gain,
        q_gain,
        k_gain,
        ffn_gain,
        w_qkv,
        w_out,
        w_router,
        w_gate_up,
        w_down,
        cotangent,
    ):
        micro = hidden_in.shape[0]
        rows = hidden_in.shape[2]
        width = hidden_in.shape[3]
        heads = HEADS
        head = width // heads
        my_heads = heads // n_w
        cols = width // n_w
        experts = w_router.shape[1]
        local_experts = w_gate_up.shape[0]
        units = w_down.shape[1]
        own = micro * rows
        seq = n_w * rows
        me = lax.axis_index("expert")
        shard = lax.axis_index("wshard")
        scale = head ** (-0.5)

        piece = width // n_w // n_e
        mine = lax.dynamic_slice_in_dim(w_qkv, me * piece, piece, 0)
        mine = mine.reshape(piece, 3, n_w, cols).transpose(2, 0, 1, 3).reshape(n_w, piece, 3 * cols)
        bank = line_exchange(
            lambda t: lax.dynamic_index_in_dim(mine, t, 0, keepdims=False), shard
        )
        upstream = cotangent.reshape(own, width)
        tokens = hidden_in.reshape(own, width).astype(F32)
        scale_one = rms_scale(tokens)
        normed = (tokens * scale_one * attn_gain).astype(LOW)
        used = jnp.any(
            routes.reshape(own, -1, 1) == jnp.arange(experts, dtype=jnp.int32), axis=1
        ).astype(LOW)
        blocks = line_gather(normed)

        rounds = max(1, n_e * n_w * own // 2 // ROUND_TOKENS)
        step = own // rounds
        hidden = units * local_experts // n_w
        arrived = (shard - jnp.arange(n_w, dtype=jnp.int32) + n_w) % n_w
        same = [[2 * c + k for c in range(n_e // 2)] for k in range(2)]
        router_rows = w_router.size // width
        used_rows = step * experts // width

        def rows_for(at):
            rows = [upstream[at : at + step], used[at : at + step].reshape(-1, width)]
            rows = jnp.concatenate(rows + [w_router.reshape(-1, width)], 0)
            return jnp.pad(rows, ((0, -rows.shape[0] % 16), (0, 0)))

        def to_line(rows):
            return lax.all_gather(rows, "wshard")

        def to_pairs(rows):
            rows = lax.all_gather(rows, "expert", axis_index_groups=same)
            return rows.reshape((-1,) + rows.shape[2:])

        pieces = [
            pack_half((shard + k) % n_w, w_gate_up, w_down, n_w // local_experts)
            for k in range(n_w)
        ]
        out_slice = lax.dynamic_slice_in_dim(w_out, me * piece, piece, 0)
        blocks, bank, dy_rows, pieces, out_slice = both(blocks, bank, rows_for(0), pieces, out_slice)

        full_out = line_gather(out_slice)
        first, second = jnp.split(pieces[2], 2, 0)
        first = shift(first, 2)
        normed_all = jnp.concatenate(blocks, 0)

        half = piece // 2
        helds = []
        for p in range(2):
            held = bank[:, p * half : (p + 1) * half]
            for d in plane[p:] + plane[:p]:
                held = joined(held, d, me)
            helds.append(held)
        helds, full_out = both(helds, full_out)
        w_heads = []
        for p, held in enumerate(helds):
            held = joined(held, 1, me)
            dims = plane[p:] + plane[:p] + [1]
            at = {d: len(dims) - 1 - k for k, d in enumerate(dims)}
            k = len(dims)
            w_heads.append(held.transpose(k, *[at[d] for d in reversed(bits)], k + 1, k + 2))
        w_heads = jnp.stack(w_heads, 1 + len(bits)).reshape(width, 3 * cols)
        full_out = jnp.split(jnp.roll(jnp.stack(full_out), shard, axis=0), 2, -1)
        ways = [plane[p:] + plane[:p] + [1] for p in range(2)]
        for step_at, (d0, d1) in enumerate(zip(*ways)):
            full_out = [joined(full_out[0], d0, me), joined(full_out[1], d1, me)]
            if step_at == 0:
                w_heads, full_out, first, dy_rows = both(w_heads, full_out, first, dy_rows)
                dy_rows = to_line(dy_rows)
                break
        orders = [list(reversed(w)) for w in ways]

        projected = mm(normed_all, w_heads)
        projected, full_out = both(projected, full_out)
        for d0, d1 in list(zip(*ways))[1:]:
            full_out = [joined(full_out[0], d0, me), joined(full_out[1], d1, me)]
        squares = jnp.sum(projected.reshape(-1, 3, cols)[:, :2] ** 2, axis=-1).T
        scales = lax.rsqrt(line_sum(squares, shard) / width + EPS)
        scales = scales.reshape(2, -1).T
        projected = projected.reshape(n_w, micro, rows, 3 * cols)
        gains = [lax.dynamic_slice_in_dim(g, shard * cols, cols) for g in (q_gain, k_gain)]
        gains = jnp.stack(gains)
        block_at = (shard + jnp.arange(n_w, dtype=jnp.int32)) % n_w
        positions = block_at[:, None] * rows + jnp.arange(rows, dtype=jnp.int32)[None, :]
        positions = positions.reshape(seq)
        freq = THETA ** (-(jnp.arange(head // 2, dtype=F32) * 2.0 / head))
        angle = positions.astype(F32)[:, None] * freq
        cosine, sine = jnp.cos(angle), jnp.sin(angle)
        cosine = jnp.concatenate([cosine, cosine], 1)
        sine = jnp.concatenate([-sine, sine], 1)
        docs = jnp.take(doc_ids[:, 0], positions, axis=1)
        mask = (positions[None, :] <= positions[:, None])[None] & (
            docs[:, :, None] == docs[:, None, :]
        )
        mask = mask.astype(F32)
        attention = functools.partial(
            attention_call,
            projected,
            scales.reshape(n_w, micro, rows, 2),
            gains,
            cosine,
            sine,
            mask,
        )
        attended = attention().reshape(n_w, own, cols)
        attended, dy_rows, full_out = both(attended, dy_rows, full_out)
        dy_all = to_pairs(dy_rows)
        attended = [shift(attended[r], r) if r else attended[r] for r in range(n_w)]
        resid, ffn_in = out_call(
            out_kernel,
            "out",
            arrived,
            [hidden_in.reshape(own, width), ffn_gain[None]] + attended,
            full_out,
            orders,
            [jax.ShapeDtypeStruct((own, width), F32), jax.ShapeDtypeStruct((own, width), LOW)],
        )

        lanes = -(-experts // 128) * 128
        expert_at = jnp.arange(lanes, dtype=jnp.int32)
        my_expert = local_experts * me + shard * local_experts // n_w
        sib_expert = local_experts * jnp.bitwise_xor(me, 1) + shard * local_experts // n_w
        hots = jnp.stack([(expert_at == e).astype(F32) for e in (my_expert, sib_expert)])

        def whole(groups):
            return jnp.concatenate([b for group in groups for _, b in group], 0)

        dffn, mixture = [], []
        grads = None
        for n in range(rounds):
            at = n * step
            ffn_rows = ffn_in[at : at + step]
            if n:
                ffn_rows, grads, dffn, mixture = lax.optimization_barrier(
                    (ffn_rows, grads, dffn, mixture)
                )
                dy_all = to_pairs(to_line(tie(rows_for(at), ffn_rows)))
            parts = pair_parts(ffn_rows, shard)
            if n == 0:
                parts, pieces, second = both(parts, pieces, second)
                pieces[1] = shift(pieces[1], 1)
            mask = dy_all[:, step : step + used_rows].reshape(-1, experts)
            mask = jnp.pad(mask, ((0, 0), (0, lanes - experts)))
            router = dy_all[:n_w, step + used_rows : step + used_rows + router_rows]
            router = jnp.pad(router.reshape(width, experts), ((0, 0), (0, lanes - experts)))
            groups, (mask, router, router_t, pieces) = plane_gather(
                parts, (mask, router, router.T, pieces)
            )
            waves = [groups]
            xs = [whole(wave) for wave in waves]
            places = [
                jnp.stack(
                    [
                        jnp.bitwise_xor(me // 2, m // 2) * (n_w // 2)
                        + jnp.bitwise_xor(shard // 2, p)
                        for group in wave
                        for p in range(2)
                        for m in group[p][0]
                    ]
                )
                for wave in waves
            ]
            if n == 0:
                pieces[3] = shift(pieces[3], 3)
                pieces[2] = jnp.concatenate([first, shift(second, 2)], 0)
                packs = [pieces, [swap(piece, 1) for piece in pieces]]
            mix = jnp.zeros((0, width), LOW)
            back, passed = [], []
            for wave, x, place in zip(waves, xs, places):
                mix, part, *rest = expert_pass(
                    x, dy_all, step, mask, hots, (router, router_t), packs, arrived, place, mix, experts
                )
                cuts = []
                for group in wave:
                    for p in range(2):
                        cuts.append((cuts[-1] if cuts else 0) + group[p][1].shape[0])
                part = jnp.split(part, cuts[:-1], 0)
                back += [part[2 * g : 2 * g + 2] for g in range(len(wave))]
                passed.append([x] + rest)
            kind = LOW if rounds == 1 else F32
            def weight_grads():
                sib = [[x, dy, dgu1, gated1, dl] for x, dy, dl, _, dgu1, _, gated1 in passed]
                own_half = [[x, dy, dgu0, gated0] for x, dy, _, dgu0, _, gated0, _ in passed]
                early = grad_pass(sib, shard, n_w, kind, 1, 1)
                early += grad_pass(own_half, shard, n_w, kind, 1, 1)
                sent = None
                if rounds == 1:
                    sent = early[2][0].astype(F32) + swap(early[0][0], 1).astype(F32)
                    sent = shift(sent.astype(LOW), 1)
                middle = grad_pass(sib, shard, n_w, kind, 3, n_w - 2)
                middle += grad_pass(own_half, shard, n_w, kind, 3, n_w - 2)
                if rounds == 1:
                    middle = (swap(middle[0], 1),) + middle[1:]
                late = grad_pass(sib, shard, n_w, kind, 2, 1)
                late += grad_pass(own_half, shard, n_w, kind, 2, 1)
                return [early, middle, late], sent

            back, (new, sent) = plane_scatter(back, weight_grads)
            grads = new if grads is None else jax.tree.map(jnp.add, grads, new)
            if n == rounds - 1:
                (sib1, router1, own1), (sib3, router3, own3), (sib2, router2, own2) = grads
                sib2 = swap(sib2.astype(LOW), 1)
                if sent is None:
                    sent = own1[0].astype(F32) + swap(sib1[0].astype(LOW), 1).astype(F32)
                    sent = shift(sent.astype(LOW), 1)
                    sib3 = swap(sib3.astype(LOW), 1)

                def added(a, b):
                    return (a.astype(F32) + b.astype(F32)).astype(LOW)

                sums = [added(own3[1], sib3[1]), sent, added(own2[0], sib2[0])]
                sums.append(added(own3[0], sib3[0]))
                third, fourth = jnp.split(sums[3], 2, 0)
                third = shift(third, 3)
                back, third = both(back, third)
                grad_router = jnp.concatenate([router3[1:], router1, router2, router3[:1]], 0)
                grad_router = jnp.roll(grad_router[..., :experts], shard, axis=0)
                grad_router = grad_router.reshape(width, experts)
            back, mix = both(back, mix)
            dffn.append(pair_scatter(back, shard))
            mixture.append(
                lax.psum_scatter(mix, "expert", axis_index_groups=same, tiled=True)
            )
        dffn = jnp.concatenate(dffn, 0)

        piece_type = jax.ShapeDtypeStruct((own, cols), LOW)
        dresid, dbranch, grad_ffn_gain, *dattended = out_call(
            out_back_kernel,
            "out_back",
            arrived,
            [dffn, resid, upstream, ffn_gain[None]],
            full_out,
            orders,
            [
                jax.ShapeDtypeStruct((own, width), F32),
                jax.ShapeDtypeStruct((own, width), LOW),
                jax.ShapeDtypeStruct((1, width), F32),
            ]
            + [piece_type] * n_w,
        )
        dattended = [shift(x, n_w - r) if r else x for r, x in enumerate(dattended)]
        dattended = jnp.concatenate(dattended, 0)
        dq, dk, dv, inners, grad_gains = attention(dattended.reshape(n_w, micro, rows, cols))
        dbranch, inners = both(dbranch, inners)
        (grad_out,) = out_call(
            out_grad_kernel,
            "out_grad",
            arrived,
            [dbranch] + attended,
            [],
            orders,
            [jax.ShapeDtypeStruct((width, width), LOW)],
        )
        inners = line_sum(jnp.sum(inners, 0).reshape(-1, 2).T, shard) / width
        inners, fourth = both(inners, fourth)
        fourth = shift(fourth, 3)
        inners = inners.reshape(2, -1).T
        flat = projected.reshape(-1, 3 * cols)
        dproj = jnp.concatenate(
            [
                norm_back(
                    flat[:, p * cols : (p + 1) * cols],
                    scales[:, p : p + 1],
                    gains[p],
                    d.reshape(-1, cols),
                    inners[:, p : p + 1],
                ).astype(LOW)
                for p, d in enumerate((dq, dk))
            ]
            + [dv.reshape(-1, cols)],
            1,
        )
        dnormed = mm_t(dproj, w_heads).astype(LOW)
        dnormed, fourth = both(dnormed, fourth)
        sums[3] = jnp.concatenate([third, fourth], 0)
        dnormed = dnormed.reshape(n_w, own, width)
        dnormed = line_scatter([dnormed[r] for r in range(n_w)])
        dnormed, sums[2], grad_out, dproj, mixture = both(
            dnormed, sums[2], grad_out, dproj, mixture
        )
        mixture = [lax.psum_scatter(m, "wshard", tiled=True).astype(F32) for m in mixture]
        sums[2] = shift(sums[2], 2)
        small = width // (n_e * n_w)
        out_part = hyper_scatter(grad_out.reshape(n_e, n_w * small, width), me, LOW, nd)
        out_part = out_part.reshape(n_w, small, width)
        out_rows = 0.0
        for k in range(n_w):
            block = lax.dynamic_index_in_dim(out_part, (shard + k) % n_w, 0, keepdims=False)
            out_rows = out_rows + (shift(block, k) if k else block).astype(F32)
        inner = jnp.mean(tokens * (attn_gain * dnormed), axis=-1, keepdims=True)
        dx = norm_back(tokens, scale_one, attn_gain, dnormed, inner)
        grad_in = (dresid + dx).astype(LOW)
        mixture = jnp.concatenate(mixture, 0)
        hidden_out = (resid + mixture).astype(LOW)
        grad_qkv = t_mm(normed_all, dproj)
        grad_attn_gain = jnp.sum(grad_qkv * w_heads.astype(F32), axis=1) / attn_gain

        qkv = hyper_scatter(grad_qkv.reshape(n_e, n_w * small, 3 * cols), me, LOW, nd)
        qkv, sums[2] = both(qkv.reshape(n_w, small, 3 * cols), sums[2])
        arrivals = []
        for k in range(n_w):
            rows_k = lax.dynamic_index_in_dim(qkv, (shard + k) % n_w, 0, keepdims=False)
            arrivals.append(shift(rows_k, k) if k else rows_k)
        out_qkv = spread(arrivals, shard)
        out_gate_up, out_down = unpack(sums, shard, local_experts)
        def all_scatter(x):
            x = x.reshape(-1, n_e, n_w * small).transpose(1, 0, 2)
            x = hyper_scatter(x, me, F32).reshape(-1, n_w, small)
            total = lax.dynamic_index_in_dim(x, shard, 1, keepdims=False)
            for s in range(1, n_w):
                send = lax.dynamic_index_in_dim(x, (shard + s) % n_w, 1, keepdims=False)
                total = total + shift(send, s)
            return total

        gains = jnp.zeros((2, width), F32)
        gains = lax.dynamic_update_slice(gains, jnp.sum(grad_gains, 0), (0, shard * cols))
        pack = [gains, grad_attn_gain[None], grad_ffn_gain, grad_router.T]
        pack, dnormed = both(jnp.concatenate(pack, 0), dnormed)
        pack = all_scatter(pack)
        return (
            hidden_out.reshape(micro, 1, rows, width),
            grad_in.reshape(micro, 1, rows, width),
            pack[2],
            pack[0],
            pack[1],
            pack[3],
            out_qkv,
            out_rows,
            pack[4:].T,
            out_gate_up,
            out_down,
        )

    return local


def solution(mesh):
    in_specs = (
        P(None, "expert", "wshard", None),
        P(None, "expert", None),
        P(None, "expert", "wshard", None),
        P(),
        P(),
        P(),
        P(),
        P("wshard", None),
        P("wshard", None),
        P("wshard", None),
        P("expert", "wshard", None),
        P("expert", None, "wshard"),
        P(None, "expert", "wshard", None),
    )
    out_specs = (
        P(None, "expert", "wshard", None),
        P(None, "expert", "wshard", None),
        P(("expert", "wshard")),
        P(("expert", "wshard")),
        P(("expert", "wshard")),
        P(("expert", "wshard")),
        P(("expert", "wshard"), None),
        P(("expert", "wshard"), None),
        P(("expert", "wshard"), None),
        P("expert", "wshard", None),
        P("expert", None, "wshard"),
    )
    local = build(mesh.shape["expert"], mesh.shape["wshard"])
    return jax.shard_map(local, mesh=mesh, in_specs=in_specs, out_specs=out_specs, check_vma=False)
```
